1024 devices in a mesh: blk: 512 (over z, y, x_hi, core), group: 2 (over x_lo).
Axes of the slice: x: 4 (x_hi: 2, x_lo: 2; x = x_hi * 2 + x_lo), y: 4, z: 32, core: 2. Of those that a mesh axis runs over, the one named last changes fastest.
Arguments:
- image_feats: bfloat16 [131072, 768], P(('blk', 'group')), may hold values from -0.796875 to 0.796875
- text_feats: bfloat16 [131072, 768], P(('blk', 'group')), may hold values from -0.796875 to 0.796875
- image_proj: bfloat16 [768, 768], replicated, may hold values from -0.21875 to 0.21875
- text_proj: bfloat16 [768, 768], replicated, may hold values from -0.21875 to 0.21875
- logit_scale: float32 [1], replicated, may hold values from 5 to 20
- logit_bias: float32 [1], replicated, may hold values from -3 to 0
- match: int32 [131072], P(('blk', 'group')), may hold values from 0 to 131071, as said below
Outputs:
- grad_image_feats: bfloat16 [131072, 768], P(('blk', 'group'))
- grad_text_feats: bfloat16 [131072, 768], P(('blk', 'group'))
The draws below stay inside these ranges and needn't reach their ends.
Inputs may be any that keep to these rules, and one draw needn't show every extreme that they name: match of an image row in block b (rows b * 2 * 128 to (b + 1) * 2 * 128 - 1) names a report row of one of the blocks (b - k) mod 512, k below 4.
All inputs are finite; a program needn't handle non-finite values.
Results may differ from the reference program's by a relative error of at most 0.02.
Values may be sent and summed in bfloat16 or wider, within the bound.
No kernel may reach another device: no remote copies, remote signals or barrier semaphores. Data moves between devices by JAX's collectives and lax.ppermute only.
A program may use at most 32 MiB of HBM per device.

```python
import math
import jax
import jax.numpy as jnp
from jax import lax

D = 768
ROWS = 128
SPAN = 4
IMAGES = 131072
N_BLK = 512
N_GROUP = 2


def draw_match(key, part):
    key = jax.random.fold_in(key, 11)
    total = ROWS * N_GROUP * N_BLK
    first, second, third = jax.random.split(key, 3)
    row_ids = jnp.arange(total, dtype=jnp.int32)
    block = row_ids // (N_GROUP * ROWS)
    back = jax.random.randint(first, (total,), 0, SPAN, dtype=jnp.int32)
    side = jax.random.randint(second, (total,), 0, N_GROUP, dtype=jnp.int32)
    offset = jax.random.randint(third, (total,), 0, ROWS, dtype=jnp.int32)
    back = jnp.where(row_ids == 0, jnp.int32(1), jnp.where(row_ids == 1, jnp.int32(0), back))
    side = jnp.where(row_ids == 0, jnp.int32(N_GROUP - 1), jnp.where(row_ids == 1, jnp.int32(0), side))
    offset = jnp.where(row_ids == 0, jnp.int32(ROWS - 1), jnp.where(row_ids == 1, jnp.int32(0), offset))
    return (((block - back) % N_BLK * N_GROUP + side) * ROWS + offset).astype(jnp.int32)


def block_scale(rng, shape, cuts, low, high):
    def one(position, parts):
        steps = jax.random.uniform(jax.random.fold_in(jax.random.fold_in(rng, 6), position), (parts,), jnp.float32, low / len(cuts), high / len(cuts))
        return jnp.repeat(jnp.exp(steps), shape[position] // parts).reshape((-1,) + (1,) * (len(shape) - position - 1))

    loudness = one(*cuts[0])
    for cut in cuts[1:]:
        loudness = loudness * one(*cut)
    return loudness


def scatter_about(stream_key, dims, scale, bound, pieces=(), kind=jnp.bfloat16):
    result = scale * jax.random.normal(stream_key, dims, jnp.float32)
    if pieces:
        result = result * block_scale(stream_key, dims, pieces, -0.22, 0.18)
    return jnp.clip(result, -bound, bound).astype(kind)


def setup_inputs(seed: int = 0) -> dict:
    splits = jax.random.split(jax.random.key(seed), 8)
    return {
        "image_feats": scatter_about(splits[0], (IMAGES, D), 0.1, 0.796875, ((0, 1024),)),
        "text_feats": scatter_about(splits[1], (IMAGES, D), 0.1, 0.796875, ((0, 1024),)),
        "image_proj": scatter_about(splits[2], (D, D), D ** -0.5, 0.21875),
        "text_proj": scatter_about(splits[3], (D, D), D ** -0.5, 0.21875),
        "logit_scale": jnp.clip(jnp.exp(jax.random.uniform(splits[4], (1,), jnp.float32, math.log(5.0), math.log(20.0))), 5.0, 20.0),
        "logit_bias": jnp.clip(jax.random.uniform(splits[5], (1,), jnp.float32, -3.0, 0.0), -3.0, 0.0),
        "match": draw_match(jax.random.fold_in(splits[7], 71), 0),
    }


def embed(feats, proj):
    x = jnp.dot(feats, proj, preferred_element_type=jnp.float32)
    inv = lax.rsqrt(lax.optimization_barrier(jnp.sum(x * x, axis=-1, keepdims=True)) + 1e-06)
    return (x * inv, inv)

def back_norm(grad, unit, inv, proj):
    inner = lax.optimization_barrier(jnp.sum(grad * unit, axis=-1, keepdims=True))
    grad_x = (inv * (grad - inner * unit)).astype(jnp.bfloat16)
    out = lax.dot_general(grad_x, proj, (((1,), (1,)), ((), ())), preferred_element_type=jnp.float32)
    return out.astype(jnp.bfloat16)

def reference(image_feats, text_feats, image_proj, text_proj, logit_scale, logit_bias, match):
    image_unit, image_inv = embed(image_feats, image_proj)
    text_unit, text_inv = embed(text_feats, text_proj)
    width_rows = N_GROUP * ROWS
    image_emb = image_unit.astype(jnp.bfloat16).reshape(N_BLK, width_rows, D).astype(jnp.float32)
    text_emb = text_unit.astype(jnp.bfloat16).reshape(N_BLK, width_rows, D).astype(jnp.float32)
    match_blocks = match.reshape(N_BLK, width_rows)
    scale = logit_scale[0]
    bias = logit_bias[0]
    block_ids = jnp.arange(N_BLK, dtype=jnp.int32)
    local_ids = jnp.arange(width_rows, dtype=jnp.int32)
    grad_image = jnp.zeros((N_BLK, width_rows, D), jnp.float32)
    grad_text = jnp.zeros((N_BLK, width_rows, D), jnp.float32)
    for step in range(SPAN):
        visiting = jnp.roll(text_emb, step, axis=0)
        source = ((block_ids - step) % N_BLK).astype(jnp.int32)
        text_ids = source[:, None] * width_rows + local_ids[None, :]
        sign = jnp.where(match_blocks[:, :, None] == text_ids[:, None, :], jnp.float32(1.0), jnp.float32(-1.0))
        logits = scale * jnp.einsum('bid,bjd->bij', image_emb, visiting) + bias
        coef = (-sign * jax.nn.sigmoid(-sign * logits) * scale).astype(jnp.bfloat16).astype(jnp.float32)
        grad_image = grad_image + jnp.einsum('bij,bjd->bid', coef, visiting)
        term = jnp.einsum('bij,bid->bjd', coef, image_emb)
        grad_text = grad_text + jnp.roll(term, -step, axis=0)
    grad_image = grad_image.reshape(N_BLK * width_rows, D)
    grad_text = grad_text.reshape(N_BLK * width_rows, D)
    return (back_norm(grad_image, image_unit, image_inv, image_proj), back_norm(grad_text, text_unit, text_inv, text_proj))
```

```python
import jax
import jax.numpy as jnp
from jax import lax
from jax.sharding import PartitionSpec as P

AXES = ("blk", "group")
KEY_ROWS = 16


def embed(feats, proj):
    x = jnp.dot(feats, proj, preferred_element_type=jnp.float32)
    inv = lax.rsqrt(jnp.sum(x * x, axis=-1, keepdims=True) + 1e-06)
    return (x * inv, inv)


def back_norm(grad, unit, inv, proj):
    inner = jnp.sum(grad * unit, axis=-1, keepdims=True)
    grad_x = (inv * (grad - inner * unit)).astype(jnp.bfloat16)
    out = lax.dot_general(
        grad_x, proj, (((1,), (1,)), ((), ())), preferred_element_type=jnp.float32
    )
    return out.astype(jnp.bfloat16)


def split_key(ids):
    return ((ids >> 8) & 255).astype(jnp.bfloat16), (ids & 255).astype(jnp.bfloat16)


def key_block(high, low, width):
    rows = jnp.stack([high, low])
    return jnp.pad(rows, ((0, KEY_ROWS - 2), (0, width - rows.shape[1])))


def joined_key(high, low):
    return high.astype(jnp.float32) * 256.0 + low.astype(jnp.float32)


def body(image_feats, text_feats, image_proj, text_proj, logit_scale, logit_bias, match):
    rows, width = image_feats.shape
    blk_count = lax.axis_size("blk")
    pair_count = blk_count // 2
    block = lax.axis_index("blk")
    half = lax.axis_index("group")
    core = block % 2
    on_text = core == 0

    def route(target):
        pairs = []
        for b in range(blk_count):
            for h in range(2):
                s, c, g = target(b // 2, b % 2, h)
                pairs.append((2 * b + h, 2 * (2 * (s % pair_count) + c) + g))
        return pairs

    def forward(core_id):
        return 1 if core_id == 0 else -1

    def flip(x):
        return lax.ppermute(x, AXES, route(lambda s, c, h: (s, 1 - c, h)))

    def swap_or_next(x):
        return lax.ppermute(
            x, AXES, route(lambda s, c, h: (s, c, 1 - h) if c == 0 else (s - 1, c, 1 - h))
        )

    def next_or_swap(x):
        return lax.ppermute(
            x, AXES, route(lambda s, c, h: (s + 1, c, 1 - h) if c == 0 else (s, c, 1 - h))
        )

    def second_next(x, cross):
        return lax.ppermute(
            x,
            AXES,
            route(lambda s, c, h: (s + 2 * forward(c), c, 1 - h if cross else h)),
        )

    high, low = split_key(match)
    raw = jnp.concatenate([image_feats, text_feats, key_block(high, low, width)])
    other = flip(raw)
    images = jnp.concatenate([image_feats, other[:rows]])
    texts = jnp.concatenate([text_feats, other[rows : 2 * rows]])
    image_unit, image_inv = embed(images, image_proj)
    text_unit, text_inv = embed(texts, text_proj)
    image_emb = image_unit.astype(jnp.bfloat16)
    text_emb = text_unit.astype(jnp.bfloat16)

    local = jnp.arange(rows, dtype=jnp.int32) + half * rows
    text_ids = jnp.concatenate([block * (2 * rows) + local, (block ^ 1) * (2 * rows) + local])
    text_high, text_low = split_key(text_ids)
    match_high = jnp.concatenate([high, other[2 * rows, :rows]])
    match_low = jnp.concatenate([low, other[2 * rows + 1, :rows]])

    def pick(text_value, image_value):
        return jnp.where(on_text, text_value, image_value)

    keys = key_block(pick(text_high, match_high), pick(text_low, match_low), width)
    sent = jnp.concatenate([pick(text_emb, image_emb), keys])
    row_key = pick(joined_key(match_high, match_low), joined_key(text_high, text_low))
    row_emb = pick(image_emb, text_emb)
    row_unit = pick(image_unit, text_unit)
    row_inv = pick(image_inv, text_inv)
    row_proj = pick(image_proj, text_proj)
    scale = logit_scale[0]
    bias = logit_bias[0]

    def pair_grad(row_from, row_to, cols, key_row, lane):
        col_emb = cols
        n = col_emb.shape[0]
        col_key = joined_key(key_row[0, lane : lane + n], key_row[1, lane : lane + n])
        sign = jnp.where(
            row_key[row_from:row_to, None] == col_key[None, :], jnp.float32(1.0), jnp.float32(-1.0)
        )
        logits = (
            scale
            * lax.dot_general(
                row_emb[row_from:row_to],
                col_emb,
                (((1,), (1,)), ((), ())),
                preferred_element_type=jnp.float32,
            )
            + bias
        )
        coef = (-sign * jax.nn.sigmoid(-sign * logits) * scale).astype(jnp.bfloat16)
        return jnp.dot(coef, col_emb, preferred_element_type=jnp.float32)

    first = swap_or_next(sent)
    second = next_or_swap(sent)
    third = second_next(sent[rows:], False)
    fourth = second_next(sent[rows:], True)
    fifth = next_or_swap(first)

    both = 2 * rows
    swapped = pick(first, second)
    near = pick(second, first)

    def block_grad(got, own_cols_only):
        keys_at = got[both:]
        if own_cols_only:
            top = pair_grad(0, rows, got[:rows], keys_at, 0)
            bottom = pair_grad(rows, both, got[:both], keys_at, 0)
            return jnp.concatenate([top, bottom])
        return pair_grad(0, both, got[:both], keys_at, 0)

    def last_grad(got):
        return pair_grad(0, rows, got[:rows], got[rows:], rows)

    grad = block_grad(sent, True)
    grad = grad + block_grad(swapped, True)
    grad = grad + block_grad(near, False)
    tail = last_grad(third) + last_grad(fourth)
    grad = grad + block_grad(fifth, False)
    grad = jnp.concatenate([grad[:rows] + tail, grad[rows:]])
    out = back_norm(grad, row_unit, row_inv, row_proj)
    own, given = out[:rows], flip(out[rows:])
    return pick(own, given), pick(given, own)


def solution(mesh):
    return jax.shard_map(
        body,
        mesh=mesh,
        in_specs=(
            P(AXES, None),
            P(AXES, None),
            P(),
            P(),
            P(),
            P(),
            P(AXES),
        ),
        out_specs=(P(AXES, None), P(AXES, None)),
        check_vma=False,
    )
```

```python
import functools

import jax
import jax.numpy as jnp
from jax import lax
from jax.experimental import pallas as pl
from jax.experimental.pallas import tpu as pltpu
from jax.sharding import PartitionSpec as P

AXES = ("blk", "group")
KEY_ROWS = 16
F32 = jnp.float32
BF16 = jnp.bfloat16


def rows_dot(a, b):
    return lax.dot_general(a, b, (((1,), (1,)), ((), ())), preferred_element_type=F32)


def key_tile(high, low, width):
    row = lax.broadcasted_iota(jnp.int32, (KEY_ROWS, width), 0)
    return jnp.where(row == 0, high, jnp.where(row == 1, low, 0)).astype(F32).astype(BF16)


def place():
    block = lax.axis_index("blk")
    return block, lax.axis_index("group"), lax.rem(block, 2)


def text_key_tile(block, half, rows):
    lane = lax.broadcasted_iota(jnp.int32, (KEY_ROWS, rows), 1)
    return key_tile(block & 255, half * rows + lane, rows)


def as_column(key):
    n = key.shape[1]
    eye = lax.broadcasted_iota(jnp.int32, (n, n), 0) == lax.broadcasted_iota(jnp.int32, (n, n), 1)
    return jnp.sum(jnp.where(eye, key, 0.0), axis=1, keepdims=True)


def joined_key(tile):
    return tile[0:1].astype(F32) * 256.0 + tile[1:2].astype(F32)


def pack_kernel(
    image_ref,
    text_ref,
    match_ref,
    raw_ref,
    match_vmem,
    sems,
):
    rows, width = image_ref.shape
    copies = [
        pltpu.make_async_copy(match_ref, match_vmem, sems.at[0]),
        pltpu.make_async_copy(image_ref, raw_ref.at[:rows], sems.at[1]),
        pltpu.make_async_copy(text_ref, raw_ref.at[rows : 2 * rows], sems.at[2]),
    ]
    for copy in copies:
        copy.start()
    raw_ref[2 * rows :, rows:] = jnp.zeros((KEY_ROWS, width - rows), BF16)
    copies[0].wait()
    match = match_vmem[...]
    raw_ref[2 * rows :, :rows] = key_tile((match >> 8) & 255, match & 255, rows)
    for copy in copies[1:]:
        copy.wait()


def load_kernel(raw_ref, image_proj_ref, text_proj_ref, col_proj_ref, row_proj_ref, sems):
    _, _, core = place()

    def load(col_from, row_from):
        copies = [
            pltpu.make_async_copy(col_from, col_proj_ref, sems.at[0]),
            pltpu.make_async_copy(row_from, row_proj_ref, sems.at[1]),
        ]
        for copy in copies:
            copy.start()
        for copy in copies:
            copy.wait()

    @pl.when(core == 0)
    def _():
        load(text_proj_ref, image_proj_ref)

    @pl.when(core == 1)
    def _():
        load(image_proj_ref, text_proj_ref)


def normed(feats, proj):
    x = jnp.dot(feats, proj, preferred_element_type=F32)
    inv = lax.rsqrt(jnp.sum(x * x, axis=-1, keepdims=True) + 1e-06)
    return x * inv, inv


def sent_kernel(raw_ref, other_ref, proj_ref, sent_ref, again_ref, far_ref):
    rows = (raw_ref.shape[0] - KEY_ROWS) // 2
    both = 2 * rows
    width = raw_ref.shape[1]
    block, half, core = place()
    start = pl.multiple_of((1 - core) * rows, rows)
    for n, ref in enumerate((raw_ref, other_ref)):
        unit, _ = normed(ref[pl.ds(start, rows)], proj_ref[...])
        sent_ref[n * rows : (n + 1) * rows] = unit.astype(BF16)
        sent_ref[both:, n * rows : (n + 1) * rows] = jnp.where(
            core == 0, text_key_tile(block ^ n, half, rows), ref[both:, :rows]
        )
    sent_ref[both:, both:] = jnp.zeros((KEY_ROWS, width - both), BF16)
    again_ref[...] = sent_ref[...]
    far_ref[...] = sent_ref[rows:]


def pair_grad(row_emb, row_key, col_emb, col_tile):
    scale, bias = row_key[:, 1:2], row_key[:, 2:3]
    logits = scale * rows_dot(row_emb, col_emb) + bias
    sign = jnp.where(row_key[:, :1] == joined_key(col_tile), F32(1.0), F32(-1.0))
    coef = (-sign * scale / (1.0 + jnp.exp(sign * logits))).astype(BF16)
    return jnp.dot(coef, col_emb, preferred_element_type=F32)


def own_kernel(
    raw_ref,
    other_ref,
    sent_ref,
    proj_ref,
    scale_ref,
    bias_ref,
    emb_ref,
    unit_ref,
    inv_ref,
    key_ref,
    grad_ref,
):
    rows = (raw_ref.shape[0] - KEY_ROWS) // 2
    both = 2 * rows
    block, half, core = place()
    start = pl.multiple_of(core * rows, rows)
    lane = lax.broadcasted_iota(jnp.int32, (rows, 128), 1)
    for n, ref in enumerate((raw_ref, other_ref)):
        at = slice(n * rows, (n + 1) * rows)
        unit, inv = normed(ref[pl.ds(start, rows)], proj_ref[...])
        unit_ref[at] = unit
        inv_ref[at] = jnp.broadcast_to(inv, (rows, 128))
        emb_ref[at] = unit.astype(BF16)
        tile = jnp.where(core == 0, ref[both:, :rows], text_key_tile(block ^ n, half, rows))
        scalars = jnp.where(lane == 1, scale_ref[0], bias_ref[0])
        key_ref[at] = jnp.where(lane == 0, as_column(joined_key(tile)), scalars)
    own_pairs(emb_ref, key_ref, sent_ref, grad_ref, False)


def own_pairs(emb_ref, key_ref, cols_ref, grad_ref, add):
    rows = emb_ref.shape[0] // 2
    both = 2 * rows
    top = pair_grad(emb_ref[:rows], key_ref[:rows], cols_ref[:rows], cols_ref[both:, :rows])
    bottom = pair_grad(emb_ref[rows:], key_ref[rows:], cols_ref[:both], cols_ref[both:, :both])
    if add:
        top = grad_ref[:rows] + top
        bottom = grad_ref[rows:] + bottom
    grad_ref[:rows] = top
    grad_ref[rows:] = bottom


def all_pairs(emb_ref, key_ref, cols_ref):
    both = emb_ref.shape[0]
    return pair_grad(emb_ref[...], key_ref[...], cols_ref[:both], cols_ref[both:, :both])


def after_kernel(*refs):
    pass


def far_kernel(emb_ref, key_ref, third_ref, fourth_ref, grad_ref, out_ref):
    both = emb_ref.shape[0]
    rows = both // 2
    total = grad_ref[:rows]
    for far_ref in (third_ref, fourth_ref):
        total += pair_grad(
            emb_ref[:rows], key_ref[:rows], far_ref[:rows], far_ref[rows:, rows:both]
        )
    out_ref[:rows] = total
    out_ref[rows:] = grad_ref[rows:]


def near_kernel(emb_ref, key_ref, first_ref, second_ref, grad_ref, out_ref):
    _, _, core = place()
    out_ref[...] = grad_ref[...]

    def pairs(swapped_ref, near_ref):
        own_pairs(emb_ref, key_ref, swapped_ref, out_ref, True)
        out_ref[...] += all_pairs(emb_ref, key_ref, near_ref)

    @pl.when(core == 0)
    def _():
        pairs(first_ref, second_ref)

    @pl.when(core == 1)
    def _():
        pairs(second_ref, first_ref)


def back_kernel(start, emb_ref, key_ref, cols_ref, grad_ref, unit_ref, inv_ref, proj_ref, out_ref):
    rows = out_ref.shape[0]
    both = 2 * rows
    at = slice(start, start + rows)
    grad = grad_ref[at] + pair_grad(
        emb_ref[at], key_ref[at], cols_ref[:both], cols_ref[both:, :both]
    )
    unit = unit_ref[at]
    inner = jnp.sum(grad * unit, axis=-1, keepdims=True)
    grad_x = (inv_ref[at, :1] * (grad - inner * unit)).astype(BF16)
    out_ref[...] = rows_dot(grad_x, proj_ref[...]).astype(BF16)


def choose_kernel(own_ref, given_ref, image_ref, text_ref, sems):
    _, _, core = place()

    def store(image_from, text_from):
        copies = [
            pltpu.make_async_copy(image_from, image_ref, sems.at[0]),
            pltpu.make_async_copy(text_from, text_ref, sems.at[1]),
        ]
        for copy in copies:
            copy.start()
        for copy in copies:
            copy.wait()

    @pl.when(core == 0)
    def _():
        store(own_ref, given_ref)

    @pl.when(core == 1)
    def _():
        store(given_ref, own_ref)


VMEM = pl.BlockSpec(memory_space=pltpu.VMEM)
SMEM = pl.BlockSpec(memory_space=pltpu.SMEM)
HBM = pl.BlockSpec(memory_space=pltpu.HBM)
ANY = pl.BlockSpec(memory_space=pl.ANY)


def call(kernel, in_specs, outs, out_spec=VMEM, scratch=(), aliases={}, vmem=24 * 2**20):
    where = pltpu.VMEM if out_spec is VMEM else jax.ShapeDtypeStruct
    shapes = tuple(where(shape, kind) for shape, kind in outs)
    return pl.pallas_call(
        kernel,
        out_shape=shapes,
        in_specs=in_specs,
        out_specs=tuple(out_spec for _ in shapes),
        scratch_shapes=scratch,
        input_output_aliases=aliases,
        compiler_params=pltpu.CompilerParams(vmem_limit_bytes=vmem),
        cost_estimate=pl.CostEstimate(flops=0, bytes_accessed=0, transcendentals=0),
    )


def body(image_feats, text_feats, image_proj, text_proj, logit_scale, logit_bias, match):
    rows, width = image_feats.shape
    both = 2 * rows
    blk_count = lax.axis_size("blk")
    pair_count = blk_count // 2

    def route(target):
        pairs = []
        for b in range(blk_count):
            for h in range(2):
                s, c, g = target(b // 2, b % 2, h)
                pairs.append((2 * b + h, 2 * (2 * (s % pair_count) + c) + g))
        return pairs

    def flip(x):
        return lax.ppermute(x, AXES, route(lambda s, c, h: (s, 1 - c, h)))

    def swap_or_next(x):
        return lax.ppermute(x, AXES, route(lambda s, c, h: (s - c, c, 1 - h)))

    def next_or_swap(x):
        return lax.ppermute(x, AXES, route(lambda s, c, h: (s + 1 - c, c, 1 - h)))

    def second_next(x, cross):
        return lax.ppermute(
            x, AXES, route(lambda s, c, h: (s + 2 - 4 * c, c, 1 - h if cross else h))
        )

    packet = ((both + KEY_ROWS, width), BF16)
    block_rows = ((rows, width), BF16)
    semaphores = pltpu.SemaphoreType.DMA
    def held(x):
        return pltpu.with_memory_space_constraint(x, pltpu.HBM)

    (raw,) = call(
        pack_kernel,
        [HBM] * 3,
        [packet],
        scratch=[pltpu.VMEM((1, rows), jnp.int32), semaphores((3,))],
    )(held(image_feats), held(text_feats), held(match.reshape(1, rows)))
    other = flip(raw)
    square = ((width, width), BF16)
    col_proj, row_proj = call(
        load_kernel, [ANY] + [HBM] * 2, [square] * 2, scratch=[semaphores((2,))]
    )(raw, held(image_proj), held(text_proj))
    sent, again, far = call(
        sent_kernel, [VMEM] * 3, [packet, packet, ((rows + KEY_ROWS, width), BF16)]
    )(raw, other, col_proj)

    def after(array, *others):
        return call(
            after_kernel, [ANY] * (1 + len(others)), [packet], ANY, aliases={0: 0}
        )(array, *others)[0]

    first = swap_or_next(sent)
    third = second_next(far, False)
    fourth = second_next(far, True)
    total = ((both, width), F32)
    emb, unit, inv, key, grad = call(
        own_kernel,
        [VMEM] * 4 + [SMEM] * 2,
        [((both, width), BF16), total, ((both, 128), F32), ((both, 128), F32), total],
    )(raw, other, sent, row_proj, logit_scale, logit_bias)
    second = next_or_swap(after(again, key))
    (grad,) = call(far_kernel, [VMEM] * 5, [total])(emb, key, third, fourth, grad)
    first = after(first, grad)
    fifth = next_or_swap(first)
    (grad,) = call(near_kernel, [VMEM] * 5, [total])(emb, key, first, second, grad)

    def back(start):
        return call(functools.partial(back_kernel, start), [VMEM] * 7, [block_rows])(
            emb, key, fifth, grad, unit, inv, row_proj
        )[0]

    given = flip(back(rows))
    own = back(0)
    return call(choose_kernel, [VMEM] * 2, [block_rows] * 2, HBM, [semaphores((2,))])(own, given)


def solution(mesh):
    return jax.shard_map(
        body,
        mesh=mesh,
        in_specs=(P(AXES, None), P(AXES, None), P(), P(), P(), P(), P(AXES)),
        out_specs=(P(AXES, None), P(AXES, None)),
        check_vma=False,
    )
```

```python
import functools

import jax
import jax.numpy as jnp
from jax import lax
from jax.experimental import pallas as pl
from jax.experimental.pallas import tpu as pltpu
from jax.sharding import PartitionSpec as P

AXES = ("blk", "group")
KEY_ROWS = 16
F32 = jnp.float32
BF16 = jnp.bfloat16


def rows_dot(a, b):
    return lax.dot_general(a, b, (((1,), (1,)), ((), ())), preferred_element_type=F32)


def key_tile(high, low, width):
    row = lax.broadcasted_iota(jnp.int32, (KEY_ROWS, width), 0)
    return jnp.where(row == 0, high, jnp.where(row == 1, low, 0)).astype(F32).astype(BF16)


def place():
    block = lax.axis_index("blk")
    return block, lax.axis_index("group"), lax.rem(block, 2)


def text_key_tile(block, half, rows):
    lane = lax.broadcasted_iota(jnp.int32, (KEY_ROWS, rows), 1)
    return key_tile(block & 255, half * rows + lane, rows)


def as_column(key):
    n = key.shape[1]
    eye = lax.broadcasted_iota(jnp.int32, (n, n), 0) == lax.broadcasted_iota(jnp.int32, (n, n), 1)
    return jnp.sum(jnp.where(eye, key, 0.0), axis=1, keepdims=True)


def joined_key(tile):
    return tile[0:1].astype(F32) * 256.0 + tile[1:2].astype(F32)


def pack_kernel(
    image_ref,
    text_ref,
    match_ref,
    raw_ref,
    match_vmem,
    sems,
):
    rows, width = image_ref.shape
    copies = [
        pltpu.make_async_copy(match_ref, match_vmem, sems.at[0]),
        pltpu.make_async_copy(image_ref, raw_ref.at[:rows], sems.at[1]),
        pltpu.make_async_copy(text_ref, raw_ref.at[rows : 2 * rows], sems.at[2]),
    ]
    for copy in copies:
        copy.start()
    raw_ref[2 * rows :, rows:] = jnp.zeros((KEY_ROWS, width - rows), BF16)
    copies[0].wait()
    match = match_vmem[...]
    raw_ref[2 * rows :, :rows] = key_tile((match >> 8) & 255, match & 255, rows)
    for copy in copies[1:]:
        copy.wait()


def load_kernel(raw_ref, image_proj_ref, text_proj_ref, col_proj_ref, row_proj_ref, sems):
    _, _, core = place()

    def load(col_from, row_from):
        copies = [
            pltpu.make_async_copy(col_from, col_proj_ref, sems.at[0]),
            pltpu.make_async_copy(row_from, row_proj_ref, sems.at[1]),
        ]
        for copy in copies:
            copy.start()
        for copy in copies:
            copy.wait()

    @pl.when(core == 0)
    def _():
        load(text_proj_ref, image_proj_ref)

    @pl.when(core == 1)
    def _():
        load(image_proj_ref, text_proj_ref)


def normed(feats, proj):
    x = jnp.dot(feats, proj, preferred_element_type=F32)
    inv = lax.rsqrt(jnp.sum(x * x, axis=-1, keepdims=True) + 1e-06)
    return x * inv, inv


def sent_kernel(raw_ref, other_ref, proj_ref, sent_ref, again_ref):
    rows = (raw_ref.shape[0] - KEY_ROWS) // 2
    both = 2 * rows
    width = raw_ref.shape[1]
    block, half, core = place()
    start = pl.multiple_of((1 - core) * rows, rows)
    for n, ref in enumerate((raw_ref, other_ref)):
        unit, _ = normed(ref[pl.ds(start, rows)], proj_ref[...])
        sent_ref[n * rows : (n + 1) * rows] = unit.astype(BF16)
        sent_ref[both:, n * rows : (n + 1) * rows] = jnp.where(
            core == 0, text_key_tile(block ^ n, half, rows), ref[both:, :rows]
        )
    sent_ref[both:, both:] = jnp.zeros((KEY_ROWS, width - both), BF16)
    again_ref[...] = sent_ref[...]


def pair_grad(row_emb, row_key, col_emb, col_tile):
    scale, bias = row_key[:, 1:2], row_key[:, 2:3]
    logits = scale * rows_dot(row_emb, col_emb) + bias
    sign = jnp.where(row_key[:, :1] == joined_key(col_tile), F32(1.0), F32(-1.0))
    coef = (-sign * scale / (1.0 + jnp.exp(sign * logits))).astype(BF16)
    return jnp.dot(coef, col_emb, preferred_element_type=F32)


def own_kernel(
    raw_ref,
    other_ref,
    sent_ref,
    proj_ref,
    scale_ref,
    bias_ref,
    emb_ref,
    unit_ref,
    inv_ref,
    key_ref,
    grad_ref,
):
    rows = (raw_ref.shape[0] - KEY_ROWS) // 2
    both = 2 * rows
    block, half, core = place()
    start = pl.multiple_of(core * rows, rows)
    lane = lax.broadcasted_iota(jnp.int32, (rows, 128), 1)
    for n, ref in enumerate((raw_ref, other_ref)):
        at = slice(n * rows, (n + 1) * rows)
        unit, inv = normed(ref[pl.ds(start, rows)], proj_ref[...])
        unit_ref[at] = unit
        inv_ref[at] = jnp.broadcast_to(inv, (rows, 128))
        emb_ref[at] = unit.astype(BF16)
        tile = jnp.where(core == 0, ref[both:, :rows], text_key_tile(block ^ n, half, rows))
        scalars = jnp.where(lane == 1, scale_ref[0], bias_ref[0])
        key_ref[at] = jnp.where(lane == 0, as_column(joined_key(tile)), scalars)
    own_pairs(emb_ref, key_ref, sent_ref, grad_ref, False)


def own_pairs(emb_ref, key_ref, cols_ref, grad_ref, add):
    rows = emb_ref.shape[0] // 2
    both = 2 * rows
    top = pair_grad(emb_ref[:rows], key_ref[:rows], cols_ref[:rows], cols_ref[both:, :rows])
    bottom = pair_grad(emb_ref[rows:], key_ref[rows:], cols_ref[:both], cols_ref[both:, :both])
    if add:
        top = grad_ref[:rows] + top
        bottom = grad_ref[rows:] + bottom
    grad_ref[:rows] = top
    grad_ref[rows:] = bottom


def all_pairs(emb_ref, key_ref, cols_ref):
    both = emb_ref.shape[0]
    return pair_grad(emb_ref[...], key_ref[...], cols_ref[:both], cols_ref[both:, :both])


def after_kernel(*refs):
    pass


def far_pack_kernel(sent_ref, first_ref, second_ref, far_ref):
    both = sent_ref.shape[0] - KEY_ROWS
    rows = both // 2
    _, _, core = place()

    def pack(swapped_ref):
        for n, ref in enumerate((sent_ref, swapped_ref)):
            at = slice(n * rows, (n + 1) * rows)
            far_ref[at] = ref[rows:both]
            far_ref[both:, at] = ref[both:, rows:both]

    @pl.when(core == 0)
    def _():
        pack(first_ref)

    @pl.when(core == 1)
    def _():
        pack(second_ref)

    far_ref[both:, both:] = sent_ref[both:, both:]


def near_kernel(emb_ref, key_ref, first_ref, second_ref, grad_ref, out_ref):
    _, _, core = place()
    out_ref[...] = grad_ref[...]

    def pairs(swapped_ref, near_ref):
        own_pairs(emb_ref, key_ref, swapped_ref, out_ref, True)
        out_ref[...] += all_pairs(emb_ref, key_ref, near_ref)

    @pl.when(core == 0)
    def _():
        pairs(first_ref, second_ref)

    @pl.when(core == 1)
    def _():
        pairs(second_ref, first_ref)


def back_kernel(part, emb_ref, key_ref, *refs):
    *cols_refs, grad_ref, unit_ref, inv_ref, proj_ref, out_ref = refs
    rows = out_ref.shape[0]
    both = 2 * rows
    at = slice(part * rows, (part + 1) * rows)
    grad = grad_ref[at]
    for ref in cols_refs:
        grad += pair_grad(emb_ref[at], key_ref[at], ref[:both], ref[both:, :both])
    unit = unit_ref[at]
    inner = jnp.sum(grad * unit, axis=-1, keepdims=True)
    grad_x = (inv_ref[at, :1] * (grad - inner * unit)).astype(BF16)
    out_ref[...] = rows_dot(grad_x, proj_ref[...]).astype(BF16)


def choose_kernel(own_ref, given_ref, image_ref, text_ref, sems):
    _, _, core = place()

    def store(image_from, text_from):
        copies = [
            pltpu.make_async_copy(image_from, image_ref, sems.at[0]),
            pltpu.make_async_copy(text_from, text_ref, sems.at[1]),
        ]
        for copy in copies:
            copy.start()
        for copy in copies:
            copy.wait()

    @pl.when(core == 0)
    def _():
        store(own_ref, given_ref)

    @pl.when(core == 1)
    def _():
        store(given_ref, own_ref)


VMEM = pl.BlockSpec(memory_space=pltpu.VMEM)
SMEM = pl.BlockSpec(memory_space=pltpu.SMEM)
HBM = pl.BlockSpec(memory_space=pltpu.HBM)
ANY = pl.BlockSpec(memory_space=pl.ANY)


def call(kernel, in_specs, outs, out_spec=VMEM, scratch=(), aliases={}, vmem=24 * 2**20):
    where = pltpu.VMEM if out_spec is VMEM else jax.ShapeDtypeStruct
    shapes = tuple(where(shape, kind) for shape, kind in outs)
    return pl.pallas_call(
        kernel,
        out_shape=shapes,
        in_specs=in_specs,
        out_specs=tuple(out_spec for _ in shapes),
        scratch_shapes=scratch,
        input_output_aliases=aliases,
        compiler_params=pltpu.CompilerParams(vmem_limit_bytes=vmem),
        cost_estimate=pl.CostEstimate(flops=0, bytes_accessed=0, transcendentals=0),
    )


def body(image_feats, text_feats, image_proj, text_proj, logit_scale, logit_bias, match):
    rows, width = image_feats.shape
    both = 2 * rows
    blk_count = lax.axis_size("blk")
    pair_count = blk_count // 2

    def route(target):
        pairs = []
        for b in range(blk_count):
            for h in range(2):
                s, c, g = target(b // 2, b % 2, h)
                pairs.append((2 * b + h, 2 * (2 * (s % pair_count) + c) + g))
        return pairs

    def flip(x):
        return lax.ppermute(x, AXES, route(lambda s, c, h: (s, 1 - c, h)))

    def swap_or_next(x):
        return lax.ppermute(x, AXES, route(lambda s, c, h: (s - c, c, 1 - h)))

    def next_or_swap(x):
        return lax.ppermute(x, AXES, route(lambda s, c, h: (s + 1 - c, c, 1 - h)))

    def second_next(x):
        return lax.ppermute(x, AXES, route(lambda s, c, h: (s + 2 - 4 * c, c, h)))

    packet = ((both + KEY_ROWS, width), BF16)
    block_rows = ((rows, width), BF16)
    semaphores = pltpu.SemaphoreType.DMA
    def held(x):
        return pltpu.with_memory_space_constraint(x, pltpu.HBM)

    (raw,) = call(
        pack_kernel,
        [HBM] * 3,
        [packet],
        scratch=[pltpu.VMEM((1, rows), jnp.int32), semaphores((3,))],
    )(held(image_feats), held(text_feats), held(match.reshape(1, rows)))
    other = flip(raw)
    square = ((width, width), BF16)
    col_proj, row_proj = call(
        load_kernel, [ANY] + [HBM] * 2, [square] * 2, scratch=[semaphores((2,))]
    )(raw, held(image_proj), held(text_proj))
    sent, again = call(sent_kernel, [VMEM] * 3, [packet] * 2)(raw, other, col_proj)

    def after(array, *others):
        return call(
            after_kernel, [ANY] * (1 + len(others)), [packet], ANY, aliases={0: 0}
        )(array, *others)[0]

    first = swap_or_next(sent)
    total = ((both, width), F32)
    emb, unit, inv, key, grad = call(
        own_kernel,
        [VMEM] * 4 + [SMEM] * 2,
        [((both, width), BF16), total, ((both, 128), F32), ((both, 128), F32), total],
    )(raw, other, sent, row_proj, logit_scale, logit_bias)
    second = next_or_swap(after(again, key))
    first = after(first, key)
    fifth = next_or_swap(first)
    (far,) = call(far_pack_kernel, [VMEM] * 3, [packet])(sent, first, second)
    far = second_next(far)
    (grad,) = call(near_kernel, [VMEM] * 5, [total])(emb, key, first, second, grad)
    (other_out,) = call(functools.partial(back_kernel, 1), [VMEM] * 7, [block_rows])(
        emb, key, fifth, grad, unit, inv, row_proj
    )
    given = flip(other_out)
    (own_out,) = call(functools.partial(back_kernel, 0), [VMEM] * 8, [block_rows])(
        emb, key, fifth, far, grad, unit, inv, row_proj
    )
    return call(choose_kernel, [VMEM] * 2, [block_rows] * 2, HBM, [semaphores((2,))])(
        own_out, given
    )


def solution(mesh):
    return jax.shard_map(
        body,
        mesh=mesh,
        in_specs=(P(AXES, None), P(AXES, None), P(), P(), P(), P(), P(AXES)),
        out_specs=(P(AXES, None), P(AXES, None)),
        check_vma=False,
    )
```

```python
import functools

import jax
import jax.numpy as jnp
from jax import lax
from jax.experimental import pallas as pl
from jax.experimental.pallas import tpu as pltpu
from jax.sharding import PartitionSpec as P

AXES = ("blk", "group")
KEY_ROWS = 16
F32 = jnp.float32
BF16 = jnp.bfloat16


def rows_dot(a, b):
    return lax.dot_general(a, b, (((1,), (1,)), ((), ())), preferred_element_type=F32)


def key_tile(high, low, width):
    row = lax.broadcasted_iota(jnp.int32, (KEY_ROWS, width), 0)
    return jnp.where(row == 0, high, jnp.where(row == 1, low, 0)).astype(F32).astype(BF16)


def place():
    block = lax.axis_index("blk")
    return block, lax.axis_index("group"), lax.rem(block, 2)


def text_key_tile(block, half, rows):
    lane = lax.broadcasted_iota(jnp.int32, (KEY_ROWS, rows), 1)
    return key_tile(block & 255, half * rows + lane, rows)


def as_column(key):
    n = key.shape[1]
    eye = lax.broadcasted_iota(jnp.int32, (n, n), 0) == lax.broadcasted_iota(jnp.int32, (n, n), 1)
    return jnp.sum(jnp.where(eye, key, 0.0), axis=1, keepdims=True)


def joined_key(tile):
    return tile[0:1].astype(F32) * 256.0 + tile[1:2].astype(F32)


def pack_kernel(
    image_ref,
    text_ref,
    match_ref,
    raw_ref,
    match_vmem,
    sems,
):
    rows, width = image_ref.shape
    copies = [
        pltpu.make_async_copy(match_ref, match_vmem, sems.at[0]),
        pltpu.make_async_copy(image_ref, raw_ref.at[:rows], sems.at[1]),
        pltpu.make_async_copy(text_ref, raw_ref.at[rows : 2 * rows], sems.at[2]),
    ]
    for copy in copies:
        copy.start()
    raw_ref[2 * rows :, rows:] = jnp.zeros((KEY_ROWS, width - rows), BF16)
    copies[0].wait()
    match = match_vmem[...]
    raw_ref[2 * rows :, :rows] = key_tile((match >> 8) & 255, match & 255, rows)
    for copy in copies[1:]:
        copy.wait()


def load_kernel(raw_ref, image_proj_ref, text_proj_ref, col_proj_ref, row_proj_ref, sems):
    _, _, core = place()

    def load(col_from, row_from):
        copies = [
            pltpu.make_async_copy(col_from, col_proj_ref, sems.at[0]),
            pltpu.make_async_copy(row_from, row_proj_ref, sems.at[1]),
        ]
        for copy in copies:
            copy.start()
        for copy in copies:
            copy.wait()

    @pl.when(core == 0)
    def _():
        load(text_proj_ref, image_proj_ref)

    @pl.when(core == 1)
    def _():
        load(image_proj_ref, text_proj_ref)


def normed(feats, proj):
    x = jnp.dot(feats, proj, preferred_element_type=F32)
    inv = lax.rsqrt(jnp.sum(x * x, axis=-1, keepdims=True) + 1e-06)
    return x * inv, inv


def sent_kernel(raw_ref, other_ref, proj_ref, sent_ref, last_ref):
    rows = (raw_ref.shape[0] - KEY_ROWS) // 2
    both = 2 * rows
    width = raw_ref.shape[1]
    block, half, core = place()
    start = pl.multiple_of((1 - core) * rows, rows)
    for n, ref in enumerate((raw_ref, other_ref)):
        unit, _ = normed(ref[pl.ds(start, rows)], proj_ref[...])
        sent_ref[n * rows : (n + 1) * rows] = unit.astype(BF16)
        sent_ref[both:, n * rows : (n + 1) * rows] = jnp.where(
            core == 0, text_key_tile(block ^ n, half, rows), ref[both:, :rows]
        )
    sent_ref[both:, both:] = jnp.zeros((KEY_ROWS, width - both), BF16)
    last_ref[...] = sent_ref[rows:]


def pair_grad(row_emb, row_key, col_emb, col_tile):
    scale, bias = row_key[:, 1:2], row_key[:, 2:3]
    logits = scale * rows_dot(row_emb, col_emb) + bias
    sign = jnp.where(row_key[:, :1] == joined_key(col_tile), F32(1.0), F32(-1.0))
    coef = (-sign * scale / (1.0 + jnp.exp(sign * logits))).astype(BF16)
    return jnp.dot(coef, col_emb, preferred_element_type=F32)


def own_kernel(
    raw_ref,
    other_ref,
    sent_ref,
    proj_ref,
    scale_ref,
    bias_ref,
    emb_ref,
    unit_ref,
    inv_ref,
    key_ref,
    grad_ref,
):
    rows = (raw_ref.shape[0] - KEY_ROWS) // 2
    both = 2 * rows
    block, half, core = place()
    start = pl.multiple_of(core * rows, rows)
    lane = lax.broadcasted_iota(jnp.int32, (rows, 128), 1)
    for n, ref in enumerate((raw_ref, other_ref)):
        at = slice(n * rows, (n + 1) * rows)
        unit, inv = normed(ref[pl.ds(start, rows)], proj_ref[...])
        unit_ref[at] = unit
        inv_ref[at] = jnp.broadcast_to(inv, (rows, 128))
        emb_ref[at] = unit.astype(BF16)
        tile = jnp.where(core == 0, ref[both:, :rows], text_key_tile(block ^ n, half, rows))
        scalars = jnp.where(lane == 1, scale_ref[0], bias_ref[0])
        key_ref[at] = jnp.where(lane == 0, as_column(joined_key(tile)), scalars)
    own_pairs(emb_ref, key_ref, sent_ref, grad_ref, False)


def own_pairs(emb_ref, key_ref, cols_ref, grad_ref, add):
    rows = emb_ref.shape[0] // 2
    both = 2 * rows
    top = pair_grad(emb_ref[:rows], key_ref[:rows], cols_ref[:rows], cols_ref[both:, :rows])
    bottom = pair_grad(emb_ref[rows:], key_ref[rows:], cols_ref[:both], cols_ref[both:, :both])
    if add:
        top = grad_ref[:rows] + top
        bottom = grad_ref[rows:] + bottom
    grad_ref[:rows] = top
    grad_ref[rows:] = bottom


def all_pairs(emb_ref, key_ref, cols_ref):
    both = emb_ref.shape[0]
    return pair_grad(emb_ref[...], key_ref[...], cols_ref[:both], cols_ref[both:, :both])


def after_kernel(*refs):
    pass


def near_kernel(emb_ref, key_ref, one_ref, two_ref, grad_ref, out_ref):
    out_ref[...] = grad_ref[...] + all_pairs(emb_ref, key_ref, one_ref)
    out_ref[...] += all_pairs(emb_ref, key_ref, two_ref)


def back_kernel(part, emb_ref, key_ref, *refs):
    *cols_refs, grad_ref, unit_ref, inv_ref, proj_ref, out_ref = refs
    rows = out_ref.shape[0]
    both = 2 * rows
    at = slice(part * rows, (part + 1) * rows)
    grad = grad_ref[at]
    for ref in cols_refs:
        start = max(0, both + KEY_ROWS - ref.shape[0])
        n = both - start if start or part else rows
        grad += pair_grad(emb_ref[at], key_ref[at], ref[:n], ref[both - start :, start : start + n])
    unit = unit_ref[at]
    inner = jnp.sum(grad * unit, axis=-1, keepdims=True)
    grad_x = (inv_ref[at, :1] * (grad - inner * unit)).astype(BF16)
    out_ref[...] = rows_dot(grad_x, proj_ref[...]).astype(BF16)


def choose_kernel(own_ref, given_ref, image_ref, text_ref, sems):
    _, _, core = place()

    def store(image_from, text_from):
        copies = [
            pltpu.make_async_copy(image_from, image_ref, sems.at[0]),
            pltpu.make_async_copy(text_from, text_ref, sems.at[1]),
        ]
        for copy in copies:
            copy.start()
        for copy in copies:
            copy.wait()

    @pl.when(core == 0)
    def _():
        store(own_ref, given_ref)

    @pl.when(core == 1)
    def _():
        store(given_ref, own_ref)


VMEM = pl.BlockSpec(memory_space=pltpu.VMEM)
SMEM = pl.BlockSpec(memory_space=pltpu.SMEM)
HBM = pl.BlockSpec(memory_space=pltpu.HBM)
ANY = pl.BlockSpec(memory_space=pl.ANY)


def call(kernel, in_specs, outs, out_spec=VMEM, scratch=(), aliases={}, vmem=24 * 2**20):
    where = pltpu.VMEM if out_spec is VMEM else jax.ShapeDtypeStruct
    shapes = tuple(where(shape, kind) for shape, kind in outs)
    return pl.pallas_call(
        kernel,
        out_shape=shapes,
        in_specs=in_specs,
        out_specs=tuple(out_spec for _ in shapes),
        scratch_shapes=scratch,
        input_output_aliases=aliases,
        compiler_params=pltpu.CompilerParams(vmem_limit_bytes=vmem),
        cost_estimate=pl.CostEstimate(flops=0, bytes_accessed=0, transcendentals=0),
    )


def body(image_feats, text_feats, image_proj, text_proj, logit_scale, logit_bias, match):
    rows, width = image_feats.shape
    both = 2 * rows
    blk_count = lax.axis_size("blk")
    pair_count = blk_count // 2

    def route(target):
        pairs = []
        for b in range(blk_count):
            for h in range(2):
                s, c, g = target(b // 2, b % 2, h)
                pairs.append((2 * b + h, 2 * (2 * (s % pair_count) + c) + g))
        return pairs

    def flip(x):
        return lax.ppermute(x, AXES, route(lambda s, c, h: (s, 1 - c, h)))

    def swap(x):
        return lax.ppermute(x, AXES, route(lambda s, c, h: (s, c, 1 - h)))

    def near(x):
        return lax.ppermute(x, AXES, route(lambda s, c, h: (s + 1 - 2 * c, c, 1 - h)))

    def across(x):
        return lax.ppermute(x, AXES, route(lambda s, c, h: (s + 1 - 2 * c, c, h)))

    def second_next(x):
        return lax.ppermute(x, AXES, route(lambda s, c, h: (s + 2 - 4 * c, c, h)))

    def second_across(x):
        return lax.ppermute(x, AXES, route(lambda s, c, h: (s + 2 - 4 * c, c, 1 - h)))

    packet = ((both + KEY_ROWS, width), BF16)
    block_rows = ((rows, width), BF16)
    semaphores = pltpu.SemaphoreType.DMA
    def held(x):
        return pltpu.with_memory_space_constraint(x, pltpu.HBM)

    (raw,) = call(
        pack_kernel,
        [HBM] * 3,
        [packet],
        scratch=[pltpu.VMEM((1, rows), jnp.int32), semaphores((3,))],
    )(held(image_feats), held(text_feats), held(match.reshape(1, rows)))
    other = flip(raw)
    square = ((width, width), BF16)
    col_proj, row_proj = call(
        load_kernel, [ANY] + [HBM] * 2, [square] * 2, scratch=[semaphores((2,))]
    )(raw, held(image_proj), held(text_proj))
    last_packet = ((rows + KEY_ROWS, width), BF16)
    sent, last = call(sent_kernel, [VMEM] * 3, [packet, last_packet])(raw, other, col_proj)

    def after(array, *others):
        return call(
            after_kernel, [ANY] * (1 + len(others)), [packet], ANY, aliases={0: 0}
        )(array, *others)[0]

    near_one = near(sent)
    near_two = across(sent)
    swapped = swap(sent)
    third = second_next(last)
    fourth = second_across(last)
    total = ((both, width), F32)
    emb, unit, inv, key, grad = call(
        own_kernel,
        [VMEM] * 4 + [SMEM] * 2,
        [((both, width), BF16), total, ((both, 128), F32), ((both, 128), F32), total],
    )(raw, other, sent, row_proj, logit_scale, logit_bias)
    (grad,) = call(near_kernel, [VMEM] * 5, [total])(emb, key, near_one, near_two, grad)
    (other_out,) = call(functools.partial(back_kernel, 1), [VMEM] * 7, [block_rows])(
        emb, key, swapped, grad, unit, inv, row_proj
    )
    given = flip(other_out)
    (own_out,) = call(functools.partial(back_kernel, 0), [VMEM] * 9, [block_rows])(
        emb, key, swapped, third, fourth, grad, unit, inv, row_proj
    )
    return call(choose_kernel, [VMEM] * 2, [block_rows] * 2, HBM, [semaphores((2,))])(
        own_out, given
    )


def solution(mesh):
    return jax.shard_map(
        body,
        mesh=mesh,
        in_specs=(P(AXES, None), P(AXES, None), P(), P(), P(), P(), P(AXES)),
        out_specs=(P(AXES, None), P(AXES, None)),
        check_vma=False,
    )
```

```python
import functools

import jax
import jax.numpy as jnp
from jax import lax
from jax.experimental import pallas as pl
from jax.experimental.pallas import tpu as pltpu
from jax.sharding import PartitionSpec as P

AXES = ("blk", "group")
KEY_ROWS = 16
F32 = jnp.float32
BF16 = jnp.bfloat16


def rows_dot(a, b):
    return lax.dot_general(a, b, (((1,), (1,)), ((), ())), preferred_element_type=F32)


def key_tile(high, low, width):
    row = lax.broadcasted_iota(jnp.int32, (KEY_ROWS, width), 0)
    return jnp.where(row == 0, high, jnp.where(row == 1, low, 0)).astype(F32).astype(BF16)


def place():
    block = lax.axis_index("blk")
    return block, lax.axis_index("group"), lax.rem(block, 2)


def text_key_tile(block, half, rows):
    lane = lax.broadcasted_iota(jnp.int32, (KEY_ROWS, rows), 1)
    return key_tile(block & 255, half * rows + lane, rows)


def as_column(key):
    n = key.shape[1]
    eye = lax.broadcasted_iota(jnp.int32, (n, n), 0) == lax.broadcasted_iota(jnp.int32, (n, n), 1)
    return jnp.sum(jnp.where(eye, key, 0.0), axis=1, keepdims=True)


def joined_key(tile):
    return tile[0:1].astype(F32) * 256.0 + tile[1:2].astype(F32)


def pack_kernel(
    image_ref,
    text_ref,
    match_ref,
    raw_ref,
    match_vmem,
    sems,
):
    rows, width = image_ref.shape
    copies = [
        pltpu.make_async_copy(match_ref, match_vmem, sems.at[0]),
        pltpu.make_async_copy(image_ref, raw_ref.at[:rows], sems.at[1]),
        pltpu.make_async_copy(text_ref, raw_ref.at[rows : 2 * rows], sems.at[2]),
    ]
    for copy in copies:
        copy.start()
    raw_ref[2 * rows :, rows:] = jnp.zeros((KEY_ROWS, width - rows), BF16)
    copies[0].wait()
    match = match_vmem[...]
    raw_ref[2 * rows :, :rows] = key_tile((match >> 8) & 255, match & 255, rows)
    for copy in copies[1:]:
        copy.wait()


def load_kernel(raw_ref, image_proj_ref, text_proj_ref, col_proj_ref, row_proj_ref, sems):
    _, _, core = place()

    def load(col_from, row_from):
        copies = [
            pltpu.make_async_copy(col_from, col_proj_ref, sems.at[0]),
            pltpu.make_async_copy(row_from, row_proj_ref, sems.at[1]),
        ]
        for copy in copies:
            copy.start()
        for copy in copies:
            copy.wait()

    @pl.when(core == 0)
    def _():
        load(text_proj_ref, image_proj_ref)

    @pl.when(core == 1)
    def _():
        load(image_proj_ref, text_proj_ref)


def normed(feats, proj):
    x = jnp.dot(feats, proj, preferred_element_type=F32)
    inv = lax.rsqrt(jnp.sum(x * x, axis=-1, keepdims=True) + 1e-06)
    return x * inv, inv


def sent_kernel(raw_ref, other_ref, proj_ref, sent_ref, last_ref):
    rows = (raw_ref.shape[0] - KEY_ROWS) // 2
    both = 2 * rows
    width = raw_ref.shape[1]
    block, half, core = place()
    start = pl.multiple_of((1 - core) * rows, rows)
    for n, ref in enumerate((raw_ref, other_ref)):
        unit, _ = normed(ref[pl.ds(start, rows)], proj_ref[...])
        sent_ref[n * rows : (n + 1) * rows] = unit.astype(BF16)
        sent_ref[both:, n * rows : (n + 1) * rows] = jnp.where(
            core == 0, text_key_tile(block ^ n, half, rows), ref[both:, :rows]
        )
    sent_ref[both:, both:] = jnp.zeros((KEY_ROWS, width - both), BF16)
    last_ref[...] = sent_ref[rows:]


def pair_grad(row_emb, row_key, col_emb, col_tile):
    scale, bias = row_key[:, 1:2], row_key[:, 2:3]
    logits = scale * rows_dot(row_emb, col_emb) + bias
    sign = jnp.where(row_key[:, :1] == joined_key(col_tile), F32(1.0), F32(-1.0))
    coef = (-sign * scale / (1.0 + jnp.exp(sign * logits))).astype(BF16)
    return jnp.dot(coef, col_emb, preferred_element_type=F32)


def own_kernel(
    raw_ref,
    other_ref,
    sent_ref,
    proj_ref,
    scale_ref,
    bias_ref,
    emb_ref,
    unit_ref,
    inv_ref,
    key_ref,
    grad_ref,
):
    rows = (raw_ref.shape[0] - KEY_ROWS) // 2
    both = 2 * rows
    block, half, core = place()
    start = pl.multiple_of(core * rows, rows)
    lane = lax.broadcasted_iota(jnp.int32, (rows, 128), 1)
    for n, ref in enumerate((raw_ref, other_ref)):
        at = slice(n * rows, (n + 1) * rows)
        unit, inv = normed(ref[pl.ds(start, rows)], proj_ref[...])
        unit_ref[at] = unit
        inv_ref[at] = jnp.broadcast_to(inv, (rows, 128))
        emb_ref[at] = unit.astype(BF16)
        tile = jnp.where(core == 0, ref[both:, :rows], text_key_tile(block ^ n, half, rows))
        scalars = jnp.where(lane == 1, scale_ref[0], bias_ref[0])
        key_ref[at] = jnp.where(lane == 0, as_column(joined_key(tile)), scalars)
    own_pairs(emb_ref, key_ref, sent_ref, grad_ref, False)


def own_pairs(emb_ref, key_ref, cols_ref, grad_ref, add):
    rows = emb_ref.shape[0] // 2
    both = 2 * rows
    top = pair_grad(emb_ref[:rows], key_ref[:rows], cols_ref[:rows], cols_ref[both:, :rows])
    bottom = pair_grad(emb_ref[rows:], key_ref[rows:], cols_ref[:both], cols_ref[both:, :both])
    if add:
        top = grad_ref[:rows] + top
        bottom = grad_ref[rows:] + bottom
    grad_ref[:rows] = top
    grad_ref[rows:] = bottom


def all_pairs(emb_ref, key_ref, cols_ref):
    both = emb_ref.shape[0]
    return pair_grad(emb_ref[...], key_ref[...], cols_ref[:both], cols_ref[both:, :both])


def after_kernel(*refs):
    pass


def near_kernel(emb_ref, key_ref, one_ref, two_ref, grad_ref, out_ref):
    out_ref[...] = grad_ref[...] + all_pairs(emb_ref, key_ref, one_ref)
    own_pairs(emb_ref, key_ref, two_ref, out_ref, True)


def back_kernel(part, emb_ref, key_ref, *refs):
    *cols_refs, grad_ref, unit_ref, inv_ref, proj_ref, out_ref = refs
    rows = out_ref.shape[0]
    both = 2 * rows
    at = slice(part * rows, (part + 1) * rows)
    grad = grad_ref[at]
    for ref in cols_refs:
        start = max(0, both + KEY_ROWS - ref.shape[0])
        n = both - start
        grad += pair_grad(emb_ref[at], key_ref[at], ref[:n], ref[both - start :, start : start + n])
    unit = unit_ref[at]
    inner = jnp.sum(grad * unit, axis=-1, keepdims=True)
    grad_x = (inv_ref[at, :1] * (grad - inner * unit)).astype(BF16)
    out_ref[...] = rows_dot(grad_x, proj_ref[...]).astype(BF16)


def choose_kernel(own_ref, given_ref, image_ref, text_ref, sems):
    _, _, core = place()

    def store(image_from, text_from):
        copies = [
            pltpu.make_async_copy(image_from, image_ref, sems.at[0]),
            pltpu.make_async_copy(text_from, text_ref, sems.at[1]),
        ]
        for copy in copies:
            copy.start()
        for copy in copies:
            copy.wait()

    @pl.when(core == 0)
    def _():
        store(own_ref, given_ref)

    @pl.when(core == 1)
    def _():
        store(given_ref, own_ref)


VMEM = pl.BlockSpec(memory_space=pltpu.VMEM)
SMEM = pl.BlockSpec(memory_space=pltpu.SMEM)
HBM = pl.BlockSpec(memory_space=pltpu.HBM)
ANY = pl.BlockSpec(memory_space=pl.ANY)


def call(kernel, in_specs, outs, out_spec=VMEM, scratch=(), aliases={}, vmem=24 * 2**20):
    where = pltpu.VMEM if out_spec is VMEM else jax.ShapeDtypeStruct
    shapes = tuple(where(shape, kind) for shape, kind in outs)
    return pl.pallas_call(
        kernel,
        out_shape=shapes,
        in_specs=in_specs,
        out_specs=tuple(out_spec for _ in shapes),
        scratch_shapes=scratch,
        input_output_aliases=aliases,
        compiler_params=pltpu.CompilerParams(vmem_limit_bytes=vmem),
        cost_estimate=pl.CostEstimate(flops=0, bytes_accessed=0, transcendentals=0),
    )


def body(image_feats, text_feats, image_proj, text_proj, logit_scale, logit_bias, match):
    rows, width = image_feats.shape
    both = 2 * rows
    blk_count = lax.axis_size("blk")
    pair_count = blk_count // 2

    def route(target):
        pairs = []
        for b in range(blk_count):
            for h in range(2):
                s, c, g = target(b // 2, b % 2, h)
                pairs.append((2 * b + h, 2 * (2 * (s % pair_count) + c) + g))
        return pairs

    def flip(x):
        return lax.ppermute(x, AXES, route(lambda s, c, h: (s, 1 - c, h)))

    def swap(x):
        return lax.ppermute(x, AXES, route(lambda s, c, h: (s, c, 1 - h)))

    def near(x):
        return lax.ppermute(x, AXES, route(lambda s, c, h: (s + 1 - 2 * c, c, 1 - h)))

    def across(x):
        return lax.ppermute(x, AXES, route(lambda s, c, h: (s + 1 - 2 * c, c, h)))

    def second_next(x):
        return lax.ppermute(x, AXES, route(lambda s, c, h: (s + 2 - 4 * c, c, h)))

    def second_across(x):
        return lax.ppermute(x, AXES, route(lambda s, c, h: (s + 2 - 4 * c, c, 1 - h)))

    packet = ((both + KEY_ROWS, width), BF16)
    block_rows = ((rows, width), BF16)
    semaphores = pltpu.SemaphoreType.DMA
    def held(x):
        return pltpu.with_memory_space_constraint(x, pltpu.HBM)

    (raw,) = call(
        pack_kernel,
        [HBM] * 3,
        [packet],
        scratch=[pltpu.VMEM((1, rows), jnp.int32), semaphores((3,))],
    )(held(image_feats), held(text_feats), held(match.reshape(1, rows)))
    other = flip(raw)
    square = ((width, width), BF16)
    col_proj, row_proj = call(
        load_kernel, [ANY] + [HBM] * 2, [square] * 2, scratch=[semaphores((2,))]
    )(raw, held(image_proj), held(text_proj))
    last_packet = ((rows + KEY_ROWS, width), BF16)
    sent, last = call(sent_kernel, [VMEM] * 3, [packet, last_packet])(raw, other, col_proj)

    def after(array, *others):
        return call(
            after_kernel, [ANY] * (1 + len(others)), [packet], ANY, aliases={0: 0}
        )(array, *others)[0]

    near_one = near(sent)
    swapped = swap(sent)
    near_two = across(sent)
    third = second_next(last)
    fourth = second_across(last)
    total = ((both, width), F32)
    emb, unit, inv, key, grad = call(
        own_kernel,
        [VMEM] * 4 + [SMEM] * 2,
        [((both, width), BF16), total, ((both, 128), F32), ((both, 128), F32), total],
    )(raw, other, sent, row_proj, logit_scale, logit_bias)
    (grad,) = call(near_kernel, [VMEM] * 5, [total])(emb, key, near_one, swapped, grad)
    (other_out,) = call(functools.partial(back_kernel, 1), [VMEM] * 7, [block_rows])(
        emb, key, near_two, grad, unit, inv, row_proj
    )
    given = flip(other_out)
    (own_out,) = call(functools.partial(back_kernel, 0), [VMEM] * 9, [block_rows])(
        emb, key, near_two, third, fourth, grad, unit, inv, row_proj
    )
    return call(choose_kernel, [VMEM] * 2, [block_rows] * 2, HBM, [semaphores((2,))])(
        own_out, given
    )


def solution(mesh):
    return jax.shard_map(
        body,
        mesh=mesh,
        in_specs=(P(AXES, None), P(AXES, None), P(), P(), P(), P(), P(AXES)),
        out_specs=(P(AXES, None), P(AXES, None)),
        check_vma=False,
    )
```

```python
import functools

import jax
import jax.numpy as jnp
from jax import lax
from jax.experimental import pallas as pl
from jax.experimental.pallas import tpu as pltpu
from jax.sharding import PartitionSpec as P

AXES = ("blk", "group")
KEY_ROWS = 16
F32 = jnp.float32
BF16 = jnp.bfloat16


def rows_dot(a, b):
    return lax.dot_general(a, b, (((1,), (1,)), ((), ())), preferred_element_type=F32)


def key_tile(high, low, width):
    row = lax.broadcasted_iota(jnp.int32, (KEY_ROWS, width), 0)
    return jnp.where(row == 0, high, jnp.where(row == 1, low, 0)).astype(F32).astype(BF16)


def place():
    block = lax.axis_index("blk")
    return block, lax.axis_index("group"), lax.rem(block, 2)


def text_key_tile(block, half, rows):
    lane = lax.broadcasted_iota(jnp.int32, (KEY_ROWS, rows), 1)
    return key_tile(block & 255, half * rows + lane, rows)


def as_column(key):
    n = key.shape[1]
    eye = lax.broadcasted_iota(jnp.int32, (n, n), 0) == lax.broadcasted_iota(jnp.int32, (n, n), 1)
    return jnp.sum(jnp.where(eye, key, 0.0), axis=1, keepdims=True)


def joined_key(tile):
    return tile[0:1].astype(F32) * 256.0 + tile[1:2].astype(F32)


def pack_kernel(
    image_ref,
    text_ref,
    match_ref,
    proj_ref,
    raw_ref,
    held_ref,
    match_vmem,
    sems,
):
    rows, width = image_ref.shape
    copies = [
        pltpu.make_async_copy(match_ref, match_vmem, sems.at[0]),
        pltpu.make_async_copy(image_ref, raw_ref.at[:rows], sems.at[1]),
        pltpu.make_async_copy(text_ref, raw_ref.at[rows : 2 * rows], sems.at[2]),
        pltpu.make_async_copy(proj_ref, held_ref, sems.at[3]),
    ]
    for copy in copies:
        copy.start()
    raw_ref[2 * rows :, rows:] = jnp.zeros((KEY_ROWS, width - rows), BF16)
    copies[0].wait()
    match = match_vmem[...]
    raw_ref[2 * rows :, :rows] = key_tile((match >> 8) & 255, match & 255, rows)
    for copy in copies[1:]:
        copy.wait()


def scalars_kernel(raw_ref, scale_ref, bias_ref, out_ref):
    lane = lax.broadcasted_iota(jnp.int32, out_ref.shape, 1)
    out_ref[...] = jnp.where(lane == 1, scale_ref[0], bias_ref[0])


def by_core(on_text, on_image):
    _, _, core = place()
    pl.when(core == 0)(on_text)
    pl.when(core == 1)(on_image)


def normed(feats, proj):
    x = jnp.dot(feats, proj, preferred_element_type=F32)
    inv = lax.rsqrt(jnp.sum(x * x, axis=-1, keepdims=True) + 1e-06)
    return x * inv, inv


def sent_kernel(
    raw_ref, other_ref, scalars_ref, image_proj_ref, text_proj_ref, sent_ref, last_ref
):
    rows = (raw_ref.shape[0] - KEY_ROWS) // 2
    both = 2 * rows
    width = raw_ref.shape[1]
    block, half, core = place()

    def project(start, proj_ref):
        for n, ref in enumerate((raw_ref, other_ref)):
            unit, _ = normed(ref[start : start + rows], proj_ref[...])
            sent_ref[n * rows : (n + 1) * rows] = unit.astype(BF16)

    by_core(lambda: project(rows, text_proj_ref), lambda: project(0, image_proj_ref))
    for n, ref in enumerate((raw_ref, other_ref)):
        sent_ref[both:, n * rows : (n + 1) * rows] = jnp.where(
            core == 0, text_key_tile(block ^ n, half, rows), ref[both:, :rows]
        )
    sent_ref[both:, both:] = jnp.zeros((KEY_ROWS, width - both), BF16)
    last_ref[...] = sent_ref[rows:]


def pair_grad(row_emb, row_key, col_emb, col_tile):
    scale, bias = row_key[:, 1:2], row_key[:, 2:3]
    logits = scale * rows_dot(row_emb, col_emb) + bias
    sign = jnp.where(row_key[:, :1] == joined_key(col_tile), F32(1.0), F32(-1.0))
    coef = (-sign * scale / (1.0 + jnp.exp(sign * logits))).astype(BF16)
    return jnp.dot(coef, col_emb, preferred_element_type=F32)


def own_kernel(
    raw_ref,
    other_ref,
    sent_ref,
    scalars_ref,
    near_ref,
    image_proj_ref,
    text_proj_ref,
    emb_ref,
    unit_ref,
    inv_ref,
    key_ref,
    grad_ref,
):
    rows = (raw_ref.shape[0] - KEY_ROWS) // 2
    both = 2 * rows
    block, half, core = place()
    lane = lax.broadcasted_iota(jnp.int32, (rows, 128), 1)

    def project(start, proj_ref):
        for n, ref in enumerate((raw_ref, other_ref)):
            at = slice(n * rows, (n + 1) * rows)
            unit, inv = normed(ref[start : start + rows], proj_ref[...])
            unit_ref[at] = unit
            inv_ref[at] = jnp.broadcast_to(inv, (rows, 128))
            emb_ref[at] = unit.astype(BF16)

    by_core(lambda: project(0, image_proj_ref), lambda: project(rows, text_proj_ref))
    for n, ref in enumerate((raw_ref, other_ref)):
        at = slice(n * rows, (n + 1) * rows)
        tile = jnp.where(core == 0, ref[both:, :rows], text_key_tile(block ^ n, half, rows))
        key_ref[at] = jnp.where(lane == 0, as_column(joined_key(tile)), scalars_ref[:1])
    grad_ref[...] = all_pairs(emb_ref, key_ref, near_ref)
    own_pairs(emb_ref, key_ref, sent_ref, grad_ref, True)


def own_pairs(emb_ref, key_ref, cols_ref, grad_ref, add):
    rows = emb_ref.shape[0] // 2
    both = 2 * rows
    top = pair_grad(emb_ref[:rows], key_ref[:rows], cols_ref[:rows], cols_ref[both:, :rows])
    bottom = pair_grad(emb_ref[rows:], key_ref[rows:], cols_ref[:both], cols_ref[both:, :both])
    if add:
        top = grad_ref[:rows] + top
        bottom = grad_ref[rows:] + bottom
    grad_ref[:rows] = top
    grad_ref[rows:] = bottom


def all_pairs(emb_ref, key_ref, cols_ref):
    both = emb_ref.shape[0]
    return pair_grad(emb_ref[...], key_ref[...], cols_ref[:both], cols_ref[both:, :both])


def after_kernel(*refs):
    pass


def back_kernel(part, emb_ref, key_ref, *refs):
    *cols_refs, grad_ref, unit_ref, inv_ref, image_proj_ref, text_proj_ref, out_ref = refs
    rows = out_ref.shape[0]
    both = 2 * rows
    at = slice(part * rows, (part + 1) * rows)
    grad = grad_ref[at]
    for place_in, ref in enumerate(cols_refs):
        start = max(0, both + KEY_ROWS - ref.shape[0])
        n = rows if place_in + part == 0 else both - start
        grad += pair_grad(emb_ref[at], key_ref[at], ref[:n], ref[both - start :, start : start + n])
    unit = unit_ref[at]
    inner = jnp.sum(grad * unit, axis=-1, keepdims=True)
    grad_x = (inv_ref[at, :1] * (grad - inner * unit)).astype(BF16)

    def finish(proj_ref):
        out_ref[...] = rows_dot(grad_x, proj_ref[...]).astype(BF16)

    by_core(lambda: finish(image_proj_ref), lambda: finish(text_proj_ref))


def choose_kernel(own_ref, given_ref, image_ref, text_ref, sems):
    _, _, core = place()

    def store(image_from, text_from):
        copies = [
            pltpu.make_async_copy(image_from, image_ref, sems.at[0]),
            pltpu.make_async_copy(text_from, text_ref, sems.at[1]),
        ]
        for copy in copies:
            copy.start()
        for copy in copies:
            copy.wait()

    @pl.when(core == 0)
    def _():
        store(own_ref, given_ref)

    @pl.when(core == 1)
    def _():
        store(given_ref, own_ref)


VMEM = pl.BlockSpec(memory_space=pltpu.VMEM)
SMEM = pl.BlockSpec(memory_space=pltpu.SMEM)
HBM = pl.BlockSpec(memory_space=pltpu.HBM)
ANY = pl.BlockSpec(memory_space=pl.ANY)


def call(
    kernel, in_specs, outs, out_spec=VMEM, scratch=(), aliases={}, vmem=24 * 2**20, nbytes=0
):
    where = pltpu.VMEM if out_spec is VMEM else jax.ShapeDtypeStruct
    shapes = tuple(where(shape, kind) for shape, kind in outs)
    return pl.pallas_call(
        kernel,
        out_shape=shapes,
        in_specs=in_specs,
        out_specs=tuple(out_spec for _ in shapes),
        scratch_shapes=scratch,
        input_output_aliases=aliases,
        compiler_params=pltpu.CompilerParams(vmem_limit_bytes=vmem),
        cost_estimate=pl.CostEstimate(flops=0, bytes_accessed=nbytes, transcendentals=0),
    )


def body(image_feats, text_feats, image_proj, text_proj, logit_scale, logit_bias, match):
    rows, width = image_feats.shape
    both = 2 * rows
    blk_count = lax.axis_size("blk")
    pair_count = blk_count // 2

    def route(target):
        pairs = []
        for b in range(blk_count):
            for h in range(2):
                s, c, g = target(b // 2, b % 2, h)
                pairs.append((2 * b + h, 2 * (2 * (s % pair_count) + c) + g))
        return pairs

    def flip(x):
        return lax.ppermute(x, AXES, route(lambda s, c, h: (s, 1 - c, h)))

    def swap(x):
        return lax.ppermute(x, AXES, route(lambda s, c, h: (s, c, 1 - h)))

    def near(x):
        return lax.ppermute(x, AXES, route(lambda s, c, h: (s + 1 - 2 * c, c, 1 - h)))

    def across(x):
        return lax.ppermute(x, AXES, route(lambda s, c, h: (s + 1 - 2 * c, c, h)))

    def second_next(x):
        return lax.ppermute(x, AXES, route(lambda s, c, h: (s + 2 - 4 * c, c, h)))

    def second_across(x):
        return lax.ppermute(x, AXES, route(lambda s, c, h: (s + 2 - 4 * c, c, 1 - h)))

    packet = ((both + KEY_ROWS, width), BF16)
    block_rows = ((rows, width), BF16)
    semaphores = pltpu.SemaphoreType.DMA
    def held(x):
        return pltpu.with_memory_space_constraint(x, pltpu.HBM)

    raw, text_proj = call(
        pack_kernel,
        [HBM] * 4,
        [packet, ((width, width), BF16)],
        scratch=[pltpu.VMEM((1, rows), jnp.int32), semaphores((4,))],
    )(held(image_feats), held(text_feats), held(match.reshape(1, rows)), held(text_proj))
    other = flip(raw)
    (scalars,) = call(scalars_kernel, [ANY] + [SMEM] * 2, [((8, 128), F32)])(
        raw, logit_scale, logit_bias
    )
    last_packet = ((rows + KEY_ROWS, width), BF16)
    sent, last = call(sent_kernel, [VMEM] * 5, [packet, last_packet])(
        raw, other, scalars, image_proj, text_proj
    )

    def after(array, *others):
        return call(
            after_kernel, [ANY] * (1 + len(others)), [packet], ANY, aliases={0: 0}
        )(array, *others)[0]

    near_one = near(sent)
    swapped = swap(sent)
    near_two = across(sent)
    third = second_next(last)
    fourth = second_across(last)
    total = ((both, width), F32)
    emb, unit, inv, key, grad = call(
        own_kernel,
        [VMEM] * 7,
        [((both, width), BF16), total, ((both, 128), F32), ((both, 128), F32), total],
    )(raw, other, sent, scalars, near_one, image_proj, text_proj)
    (other_out,) = call(functools.partial(back_kernel, 1), [VMEM] * 9, [block_rows])(
        emb, key, swapped, near_two, grad, unit, inv, image_proj, text_proj
    )
    given = flip(other_out)
    (own_out,) = call(functools.partial(back_kernel, 0), [VMEM] * 11, [block_rows])(
        emb, key, swapped, near_two, third, fourth, grad, unit, inv, image_proj, text_proj
    )
    return call(choose_kernel, [VMEM] * 2, [block_rows] * 2, HBM, [semaphores((2,))])(
        own_out, given
    )


def solution(mesh):
    return jax.shard_map(
        body,
        mesh=mesh,
        in_specs=(P(AXES, None), P(AXES, None), P(), P(), P(), P(), P(AXES)),
        out_specs=(P(AXES, None), P(AXES, None)),
        check_vma=False,
    )
```

```python
import functools

import jax
import jax.numpy as jnp
from jax import lax
from jax.experimental import pallas as pl
from jax.experimental.pallas import tpu as pltpu
from jax.sharding import PartitionSpec as P

AXES = ("blk", "group")
KEY_ROWS = 16
F32 = jnp.float32
BF16 = jnp.bfloat16


def rows_dot(a, b):
    return lax.dot_general(a, b, (((1,), (1,)), ((), ())), preferred_element_type=F32)


def key_tile(high, low, width):
    row = lax.broadcasted_iota(jnp.int32, (KEY_ROWS, width), 0)
    return jnp.where(row == 0, high, jnp.where(row == 1, low, 0)).astype(F32).astype(BF16)


def place():
    block = lax.axis_index("blk")
    return block, lax.axis_index("group"), lax.rem(block, 2)


def text_key_tile(block, half, rows):
    lane = lax.broadcasted_iota(jnp.int32, (KEY_ROWS, rows), 1)
    return key_tile(block & 255, half * rows + lane, rows)


def as_column(key):
    n = key.shape[1]
    eye = lax.broadcasted_iota(jnp.int32, (n, n), 0) == lax.broadcasted_iota(jnp.int32, (n, n), 1)
    return jnp.sum(jnp.where(eye, key, 0.0), axis=1, keepdims=True)


def joined_key(tile):
    return tile[0:1].astype(F32) * 256.0 + tile[1:2].astype(F32)


def pack_kernel(
    image_ref,
    text_ref,
    match_ref,
    raw_ref,
    match_vmem,
    sems,
):
    rows, width = image_ref.shape
    copies = [
        pltpu.make_async_copy(match_ref, match_vmem, sems.at[0]),
        pltpu.make_async_copy(image_ref, raw_ref.at[:rows], sems.at[1]),
        pltpu.make_async_copy(text_ref, raw_ref.at[rows : 2 * rows], sems.at[2]),
    ]
    for copy in copies:
        copy.start()
    raw_ref[2 * rows :, rows:] = jnp.zeros((KEY_ROWS, width - rows), BF16)
    copies[0].wait()
    match = match_vmem[...]
    raw_ref[2 * rows :, :rows] = key_tile((match >> 8) & 255, match & 255, rows)
    for copy in copies[1:]:
        copy.wait()


def load_kernel(raw_ref, image_proj_ref, text_proj_ref, col_proj_ref, row_proj_ref, sems):
    _, _, core = place()

    def load(col_from, row_from):
        copies = [
            pltpu.make_async_copy(col_from, col_proj_ref, sems.at[0]),
            pltpu.make_async_copy(row_from, row_proj_ref, sems.at[1]),
        ]
        for copy in copies:
            copy.start()
        for copy in copies:
            copy.wait()

    @pl.when(core == 0)
    def _():
        load(text_proj_ref, image_proj_ref)

    @pl.when(core == 1)
    def _():
        load(image_proj_ref, text_proj_ref)


def normed(feats, proj):
    x = jnp.dot(feats, proj, preferred_element_type=F32)
    inv = lax.rsqrt(jnp.sum(x * x, axis=-1, keepdims=True) + 1e-06)
    return x * inv, inv


def sent_kernel(raw_ref, other_ref, proj_ref, sent_ref, last_ref):
    rows = (raw_ref.shape[0] - KEY_ROWS) // 2
    both = 2 * rows
    width = raw_ref.shape[1]
    block, half, core = place()
    start = pl.multiple_of((1 - core) * rows, rows)
    for n, ref in enumerate((raw_ref, other_ref)):
        unit, _ = normed(ref[pl.ds(start, rows)], proj_ref[...])
        sent_ref[n * rows : (n + 1) * rows] = unit.astype(BF16)
        sent_ref[both:, n * rows : (n + 1) * rows] = jnp.where(
            core == 0, text_key_tile(block ^ n, half, rows), ref[both:, :rows]
        )
    sent_ref[both:, both:] = jnp.zeros((KEY_ROWS, width - both), BF16)
    last_ref[...] = sent_ref[rows:]


def pair_grad(row_emb, row_key, col_emb, col_tile):
    scale, bias = row_key[:, 1:2], row_key[:, 2:3]
    logits = scale * rows_dot(row_emb, col_emb) + bias
    sign = jnp.where(row_key[:, :1] == joined_key(col_tile), F32(1.0), F32(-1.0))
    coef = (-sign * scale / (1.0 + jnp.exp(sign * logits))).astype(BF16)
    return jnp.dot(coef, col_emb, preferred_element_type=F32)


def own_kernel(
    raw_ref,
    other_ref,
    sent_ref,
    near_ref,
    proj_ref,
    scale_ref,
    bias_ref,
    emb_ref,
    unit_ref,
    inv_ref,
    key_ref,
    grad_ref,
):
    rows = (raw_ref.shape[0] - KEY_ROWS) // 2
    both = 2 * rows
    block, half, core = place()
    start = pl.multiple_of(core * rows, rows)
    lane = lax.broadcasted_iota(jnp.int32, (rows, 128), 1)
    for n, ref in enumerate((raw_ref, other_ref)):
        at = slice(n * rows, (n + 1) * rows)
        unit, inv = normed(ref[pl.ds(start, rows)], proj_ref[...])
        unit_ref[at] = unit
        inv_ref[at] = jnp.broadcast_to(inv, (rows, 128))
        emb_ref[at] = unit.astype(BF16)
        tile = jnp.where(core == 0, ref[both:, :rows], text_key_tile(block ^ n, half, rows))
        scalars = jnp.where(lane == 1, scale_ref[0], bias_ref[0])
        key_ref[at] = jnp.where(lane == 0, as_column(joined_key(tile)), scalars)
    grad_ref[...] = all_pairs(emb_ref, key_ref, near_ref)
    own_pairs(emb_ref, key_ref, sent_ref, grad_ref, True)


def own_pairs(emb_ref, key_ref, cols_ref, grad_ref, add):
    rows = emb_ref.shape[0] // 2
    both = 2 * rows
    top = pair_grad(emb_ref[:rows], key_ref[:rows], cols_ref[:rows], cols_ref[both:, :rows])
    bottom = pair_grad(emb_ref[rows:], key_ref[rows:], cols_ref[:both], cols_ref[both:, :both])
    if add:
        top = grad_ref[:rows] + top
        bottom = grad_ref[rows:] + bottom
    grad_ref[:rows] = top
    grad_ref[rows:] = bottom


def all_pairs(emb_ref, key_ref, cols_ref):
    both = emb_ref.shape[0]
    return pair_grad(emb_ref[...], key_ref[...], cols_ref[:both], cols_ref[both:, :both])


def after_kernel(*refs):
    pass


def back_kernel(part, emb_ref, key_ref, *refs):
    *cols_refs, grad_ref, unit_ref, inv_ref, proj_ref, out_ref = refs
    rows = out_ref.shape[0]
    both = 2 * rows
    at = slice(part * rows, (part + 1) * rows)
    grad = grad_ref[at]
    for place_in, ref in enumerate(cols_refs):
        start = max(0, both + KEY_ROWS - ref.shape[0])
        n = rows if place_in + part == 0 else both - start
        grad += pair_grad(emb_ref[at], key_ref[at], ref[:n], ref[both - start :, start : start + n])
    unit = unit_ref[at]
    inner = jnp.sum(grad * unit, axis=-1, keepdims=True)
    grad_x = (inv_ref[at, :1] * (grad - inner * unit)).astype(BF16)
    out_ref[...] = rows_dot(grad_x, proj_ref[...]).astype(BF16)


def choose_kernel(own_ref, given_ref, image_ref, text_ref, sems):
    _, _, core = place()

    def store(image_from, text_from):
        copies = [
            pltpu.make_async_copy(image_from, image_ref, sems.at[0]),
            pltpu.make_async_copy(text_from, text_ref, sems.at[1]),
        ]
        for copy in copies:
            copy.start()
        for copy in copies:
            copy.wait()

    @pl.when(core == 0)
    def _():
        store(own_ref, given_ref)

    @pl.when(core == 1)
    def _():
        store(given_ref, own_ref)


VMEM = pl.BlockSpec(memory_space=pltpu.VMEM)
SMEM = pl.BlockSpec(memory_space=pltpu.SMEM)
HBM = pl.BlockSpec(memory_space=pltpu.HBM)
ANY = pl.BlockSpec(memory_space=pl.ANY)


def call(kernel, in_specs, outs, out_spec=VMEM, scratch=(), aliases={}, vmem=24 * 2**20):
    where = pltpu.VMEM if out_spec is VMEM else jax.ShapeDtypeStruct
    shapes = tuple(where(shape, kind) for shape, kind in outs)
    return pl.pallas_call(
        kernel,
        out_shape=shapes,
        in_specs=in_specs,
        out_specs=tuple(out_spec for _ in shapes),
        scratch_shapes=scratch,
        input_output_aliases=aliases,
        compiler_params=pltpu.CompilerParams(vmem_limit_bytes=vmem),
        cost_estimate=pl.CostEstimate(flops=0, bytes_accessed=0, transcendentals=0),
    )


def body(image_feats, text_feats, image_proj, text_proj, logit_scale, logit_bias, match):
    rows, width = image_feats.shape
    both = 2 * rows
    blk_count = lax.axis_size("blk")
    pair_count = blk_count // 2

    def route(target):
        pairs = []
        for b in range(blk_count):
            for h in range(2):
                s, c, g = target(b // 2, b % 2, h)
                pairs.append((2 * b + h, 2 * (2 * (s % pair_count) + c) + g))
        return pairs

    def flip(x):
        return lax.ppermute(x, AXES, route(lambda s, c, h: (s, 1 - c, h)))

    def swap(x):
        return lax.ppermute(x, AXES, route(lambda s, c, h: (s, c, 1 - h)))

    def near(x):
        return lax.ppermute(x, AXES, route(lambda s, c, h: (s + 1 - 2 * c, c, 1 - h)))

    def across(x):
        return lax.ppermute(x, AXES, route(lambda s, c, h: (s + 1 - 2 * c, c, h)))

    def second_next(x):
        return lax.ppermute(x, AXES, route(lambda s, c, h: (s + 2 - 4 * c, c, h)))

    def second_across(x):
        return lax.ppermute(x, AXES, route(lambda s, c, h: (s + 2 - 4 * c, c, 1 - h)))

    packet = ((both + KEY_ROWS, width), BF16)
    block_rows = ((rows, width), BF16)
    semaphores = pltpu.SemaphoreType.DMA
    def held(x):
        return pltpu.with_memory_space_constraint(x, pltpu.HBM)

    (raw,) = call(
        pack_kernel,
        [HBM] * 3,
        [packet],
        scratch=[pltpu.VMEM((1, rows), jnp.int32), semaphores((3,))],
    )(held(image_feats), held(text_feats), held(match.reshape(1, rows)))
    other = flip(raw)
    square = ((width, width), BF16)
    col_proj, row_proj = call(
        load_kernel, [ANY] + [HBM] * 2, [square] * 2, scratch=[semaphores((2,))]
    )(raw, held(image_proj), held(text_proj))
    last_packet = ((rows + KEY_ROWS, width), BF16)
    sent, last = call(sent_kernel, [VMEM] * 3, [packet, last_packet])(raw, other, col_proj)

    def after(array, *others):
        return call(
            after_kernel, [ANY] * (1 + len(others)), [packet], ANY, aliases={0: 0}
        )(array, *others)[0]

    near_one = near(sent)
    swapped = swap(sent)
    near_two = across(sent)
    third = second_next(last)
    fourth = second_across(last)
    total = ((both, width), F32)
    emb, unit, inv, key, grad = call(
        own_kernel,
        [VMEM] * 5 + [SMEM] * 2,
        [((both, width), BF16), total, ((both, 128), F32), ((both, 128), F32), total],
    )(raw, other, sent, near_one, row_proj, logit_scale, logit_bias)
    (other_out,) = call(functools.partial(back_kernel, 1), [VMEM] * 8, [block_rows])(
        emb, key, swapped, near_two, grad, unit, inv, row_proj
    )
    given = flip(other_out)
    (own_out,) = call(functools.partial(back_kernel, 0), [VMEM] * 10, [block_rows])(
        emb, key, swapped, near_two, third, fourth, grad, unit, inv, row_proj
    )
    return call(choose_kernel, [VMEM] * 2, [block_rows] * 2, HBM, [semaphores((2,))])(
        own_out, given
    )


def solution(mesh):
    return jax.shard_map(
        body,
        mesh=mesh,
        in_specs=(P(AXES, None), P(AXES, None), P(), P(), P(), P(), P(AXES)),
        out_specs=(P(AXES, None), P(AXES, None)),
        check_vma=False,
    )
```

```python
import functools

import jax
import jax.numpy as jnp
from jax import lax
from jax.experimental import pallas as pl
from jax.experimental.pallas import tpu as pltpu
from jax.sharding import PartitionSpec as P

AXES = ("blk", "group")
KEY_ROWS = 16
F32 = jnp.float32
BF16 = jnp.bfloat16


def rows_dot(a, b):
    return lax.dot_general(a, b, (((1,), (1,)), ((), ())), preferred_element_type=F32)


def key_tile(high, low, width):
    row = lax.broadcasted_iota(jnp.int32, (KEY_ROWS, width), 0)
    return jnp.where(row == 0, high, jnp.where(row == 1, low, 0)).astype(F32).astype(BF16)


def place():
    block = lax.axis_index("blk")
    return block, lax.axis_index("group"), lax.rem(block, 2)


def text_key_tile(block, half, rows):
    lane = lax.broadcasted_iota(jnp.int32, (KEY_ROWS, rows), 1)
    return key_tile(block & 255, half * rows + lane, rows)


def as_column(key):
    n = key.shape[1]
    eye = lax.broadcasted_iota(jnp.int32, (n, n), 0) == lax.broadcasted_iota(jnp.int32, (n, n), 1)
    return jnp.sum(jnp.where(eye, key, 0.0), axis=1, keepdims=True)


def joined_key(tile):
    return tile[0:1].astype(F32) * 256.0 + tile[1:2].astype(F32)


def pack_kernel(
    image_ref,
    text_ref,
    match_ref,
    raw_ref,
    match_vmem,
    sems,
):
    rows, width = image_ref.shape
    copies = [
        pltpu.make_async_copy(match_ref, match_vmem, sems.at[0]),
        pltpu.make_async_copy(image_ref, raw_ref.at[:rows], sems.at[1]),
        pltpu.make_async_copy(text_ref, raw_ref.at[rows : 2 * rows], sems.at[2]),
    ]
    for copy in copies:
        copy.start()
    raw_ref[2 * rows :, rows:] = jnp.zeros((KEY_ROWS, width - rows), BF16)
    copies[0].wait()
    match = match_vmem[...]
    raw_ref[2 * rows :, :rows] = key_tile((match >> 8) & 255, match & 255, rows)
    for copy in copies[1:]:
        copy.wait()


def load_kernel(raw_ref, image_proj_ref, text_proj_ref, col_proj_ref, row_proj_ref, sems):
    _, _, core = place()

    def load(col_from, row_from):
        copies = [
            pltpu.make_async_copy(col_from, col_proj_ref, sems.at[0]),
            pltpu.make_async_copy(row_from, row_proj_ref, sems.at[1]),
        ]
        for copy in copies:
            copy.start()
        for copy in copies:
            copy.wait()

    @pl.when(core == 0)
    def _():
        load(text_proj_ref, image_proj_ref)

    @pl.when(core == 1)
    def _():
        load(image_proj_ref, text_proj_ref)


def normed(feats, proj):
    x = jnp.dot(feats, proj, preferred_element_type=F32)
    inv = lax.rsqrt(jnp.sum(x * x, axis=-1, keepdims=True) + 1e-06)
    return x * inv, inv


def sent_kernel(raw_ref, other_ref, proj_ref, sent_ref, last_ref):
    rows = (raw_ref.shape[0] - KEY_ROWS) // 2
    both = 2 * rows
    width = raw_ref.shape[1]
    block, half, core = place()
    start = pl.multiple_of((1 - core) * rows, rows)
    for n, ref in enumerate((raw_ref, other_ref)):
        unit, _ = normed(ref[pl.ds(start, rows)], proj_ref[...])
        sent_ref[n * rows : (n + 1) * rows] = unit.astype(BF16)
        sent_ref[both:, n * rows : (n + 1) * rows] = jnp.where(
            core == 0, text_key_tile(block ^ n, half, rows), ref[both:, :rows]
        )
    sent_ref[both:, both:] = jnp.zeros((KEY_ROWS, width - both), BF16)
    last_ref[...] = sent_ref[rows:]


def pair_grad(row_emb, row_key, col_emb, col_tile):
    scale, bias = row_key[:, 1:2], row_key[:, 2:3]
    logits = scale * rows_dot(row_emb, col_emb) + bias
    paired = row_key[:, :1] == joined_key(col_tile)
    top = jnp.where(paired, -scale, scale)
    coef = (top / (1.0 + jnp.exp(jnp.where(paired, logits, -logits)))).astype(BF16)
    return jnp.dot(coef, col_emb, preferred_element_type=F32)


def own_kernel(
    raw_ref,
    other_ref,
    sent_ref,
    near_ref,
    proj_ref,
    scale_ref,
    bias_ref,
    emb_ref,
    unit_ref,
    inv_ref,
    key_ref,
    grad_ref,
):
    rows = (raw_ref.shape[0] - KEY_ROWS) // 2
    both = 2 * rows
    block, half, core = place()
    start = pl.multiple_of(core * rows, rows)
    lane = lax.broadcasted_iota(jnp.int32, (rows, 128), 1)
    for n, ref in enumerate((raw_ref, other_ref)):
        at = slice(n * rows, (n + 1) * rows)
        unit, inv = normed(ref[pl.ds(start, rows)], proj_ref[...])
        unit_ref[at] = unit
        inv_ref[at] = jnp.broadcast_to(inv, (rows, 128))
        emb_ref[at] = unit.astype(BF16)
        tile = jnp.where(core == 0, ref[both:, :rows], text_key_tile(block ^ n, half, rows))
        scalars = jnp.where(lane == 1, scale_ref[0], bias_ref[0])
        key_ref[at] = jnp.where(lane == 0, as_column(joined_key(tile)), scalars)
    grad_ref[...] = all_pairs(emb_ref, key_ref, near_ref)
    own_pairs(emb_ref, key_ref, sent_ref, grad_ref, True)


def own_pairs(emb_ref, key_ref, cols_ref, grad_ref, add):
    rows = emb_ref.shape[0] // 2
    both = 2 * rows
    top = pair_grad(emb_ref[:rows], key_ref[:rows], cols_ref[:rows], cols_ref[both:, :rows])
    bottom = pair_grad(emb_ref[rows:], key_ref[rows:], cols_ref[:both], cols_ref[both:, :both])
    if add:
        top = grad_ref[:rows] + top
        bottom = grad_ref[rows:] + bottom
    grad_ref[:rows] = top
    grad_ref[rows:] = bottom


def all_pairs(emb_ref, key_ref, cols_ref):
    both = emb_ref.shape[0]
    return pair_grad(emb_ref[...], key_ref[...], cols_ref[:both], cols_ref[both:, :both])


def after_kernel(*refs):
    pass


def back_kernel(part, emb_ref, key_ref, *refs):
    *cols_refs, grad_ref, unit_ref, inv_ref, proj_ref, out_ref = refs
    rows = out_ref.shape[0]
    both = 2 * rows
    at = slice(part * rows, (part + 1) * rows)
    grad = grad_ref[at]
    for place_in, ref in enumerate(cols_refs):
        start = max(0, both + KEY_ROWS - ref.shape[0])
        n = rows if place_in + part == 0 else both - start
        grad += pair_grad(emb_ref[at], key_ref[at], ref[:n], ref[both - start :, start : start + n])
    unit = unit_ref[at]
    inner = jnp.sum(grad * unit, axis=-1, keepdims=True)
    grad_x = (inv_ref[at, :1] * (grad - inner * unit)).astype(BF16)
    out_ref[...] = rows_dot(grad_x, proj_ref[...]).astype(BF16)


def choose_kernel(own_ref, given_ref, image_ref, text_ref, sems):
    _, _, core = place()

    def store(image_from, text_from):
        copies = [
            pltpu.make_async_copy(image_from, image_ref, sems.at[0]),
            pltpu.make_async_copy(text_from, text_ref, sems.at[1]),
        ]
        for copy in copies:
            copy.start()
        for copy in copies:
            copy.wait()

    @pl.when(core == 0)
    def _():
        store(own_ref, given_ref)

    @pl.when(core == 1)
    def _():
        store(given_ref, own_ref)


VMEM = pl.BlockSpec(memory_space=pltpu.VMEM)
SMEM = pl.BlockSpec(memory_space=pltpu.SMEM)
HBM = pl.BlockSpec(memory_space=pltpu.HBM)
ANY = pl.BlockSpec(memory_space=pl.ANY)


def call(kernel, in_specs, outs, out_spec=VMEM, scratch=(), aliases={}, vmem=24 * 2**20):
    where = pltpu.VMEM if out_spec is VMEM else jax.ShapeDtypeStruct
    shapes = tuple(where(shape, kind) for shape, kind in outs)
    return pl.pallas_call(
        kernel,
        out_shape=shapes,
        in_specs=in_specs,
        out_specs=tuple(out_spec for _ in shapes),
        scratch_shapes=scratch,
        input_output_aliases=aliases,
        compiler_params=pltpu.CompilerParams(vmem_limit_bytes=vmem),
        cost_estimate=pl.CostEstimate(flops=0, bytes_accessed=0, transcendentals=0),
    )


def body(image_feats, text_feats, image_proj, text_proj, logit_scale, logit_bias, match):
    rows, width = image_feats.shape
    both = 2 * rows
    blk_count = lax.axis_size("blk")
    pair_count = blk_count // 2

    def route(target):
        pairs = []
        for b in range(blk_count):
            for h in range(2):
                s, c, g = target(b // 2, b % 2, h)
                pairs.append((2 * b + h, 2 * (2 * (s % pair_count) + c) + g))
        return pairs

    def flip(x):
        return lax.ppermute(x, AXES, route(lambda s, c, h: (s, 1 - c, h)))

    def swap(x):
        return lax.ppermute(x, AXES, route(lambda s, c, h: (s, c, 1 - h)))

    def near(x):
        return lax.ppermute(x, AXES, route(lambda s, c, h: (s + 1 - 2 * c, c, 1 - h)))

    def across(x):
        return lax.ppermute(x, AXES, route(lambda s, c, h: (s + 1 - 2 * c, c, h)))

    def second_next(x):
        return lax.ppermute(x, AXES, route(lambda s, c, h: (s + 2 - 4 * c, c, h)))

    def second_across(x):
        return lax.ppermute(x, AXES, route(lambda s, c, h: (s + 2 - 4 * c, c, 1 - h)))

    packet = ((both + KEY_ROWS, width), BF16)
    block_rows = ((rows, width), BF16)
    semaphores = pltpu.SemaphoreType.DMA
    def held(x):
        return pltpu.with_memory_space_constraint(x, pltpu.HBM)

    (raw,) = call(
        pack_kernel,
        [HBM] * 3,
        [packet],
        scratch=[pltpu.VMEM((1, rows), jnp.int32), semaphores((3,))],
    )(held(image_feats), held(text_feats), held(match.reshape(1, rows)))
    other = flip(raw)
    square = ((width, width), BF16)
    col_proj, row_proj = call(
        load_kernel, [ANY] + [HBM] * 2, [square] * 2, scratch=[semaphores((2,))]
    )(raw, held(image_proj), held(text_proj))
    last_packet = ((rows + KEY_ROWS, width), BF16)
    sent, last = call(sent_kernel, [VMEM] * 3, [packet, last_packet])(raw, other, col_proj)

    def after(array, *others):
        return call(
            after_kernel, [ANY] * (1 + len(others)), [packet], ANY, aliases={0: 0}
        )(array, *others)[0]

    near_one = near(sent)
    swapped = swap(sent)
    near_two = across(sent)
    third = second_next(last)
    fourth = second_across(last)
    total = ((both, width), F32)
    emb, unit, inv, key, grad = call(
        own_kernel,
        [VMEM] * 5 + [SMEM] * 2,
        [((both, width), BF16), total, ((both, 128), F32), ((both, 128), F32), total],
    )(raw, other, sent, near_one, row_proj, logit_scale, logit_bias)
    (other_out,) = call(functools.partial(back_kernel, 1), [VMEM] * 8, [block_rows])(
        emb, key, swapped, near_two, grad, unit, inv, row_proj
    )
    given = flip(other_out)
    (own_out,) = call(functools.partial(back_kernel, 0), [VMEM] * 10, [block_rows])(
        emb, key, swapped, near_two, third, fourth, grad, unit, inv, row_proj
    )
    return call(choose_kernel, [VMEM] * 2, [block_rows] * 2, HBM, [semaphores((2,))])(
        own_out, given
    )


def solution(mesh):
    return jax.shard_map(
        body,
        mesh=mesh,
        in_specs=(P(AXES, None), P(AXES, None), P(), P(), P(), P(), P(AXES)),
        out_specs=(P(AXES, None), P(AXES, None)),
        check_vma=False,
    )
```
